128 devices in a mesh: patch: 16 (over y, x), head: 8 (over z, core).
Axes of the slice: x: 4, y: 4, z: 4, core: 2. Of those that a mesh axis runs over, the one named last changes fastest.
Arguments:
- hidden: bfloat16 [16384, 3072], P('patch', 'head'), may hold values from -6 to 6
- key_cache: bfloat16 [16384, 3072], P('patch', 'head'), may hold values from -600 to 600
- value_cache: bfloat16 [16384, 3072], P('patch', 'head'), may hold values from -6 to 6
- block_order: int32 [16, 8], P('patch'), may hold values from 0 to 7, each once within a row
- refresh_counts: int32 [16], P('patch'), may hold values from 1 to 4, 32 in all
- modulation: float32 [3, 3072], replicated, may hold values from -4 to 4
- query_gain: float32 [128], replicated, may hold values from 0.25 to 1.75
- key_gain: float32 [128], replicated, may hold values from 2 to 4
- w_qkv: bfloat16 [3072, 3, 3072], P(None, None, 'head'), may hold values from -0.109375 to 0.109375
- w_mlp: bfloat16 [3072, 6144], P(None, 'head'), may hold values from -0.109375 to 0.109375
- w_out_attn: bfloat16 [3072, 3072], P('head'), may hold values from -0.0625 to 0.0625
- w_out_mlp: bfloat16 [6144, 3072], P('head'), may hold values from -0.0625 to 0.0625
Outputs:
- refreshed_out: bfloat16 [8192, 3072], P('patch', 'head')
The draws below stay inside these ranges and needn't reach their ends.
Inputs may be any that keep to these rules, and one draw needn't show every extreme that they name: `block_order`: each row holds every block number of a shard once. `refresh_counts`: the counts of all shards sum to exactly 2 times the number of patch shards, and some shard has 4.
All inputs are finite; a program needn't handle non-finite values.
Results may differ from the reference program's by a relative error of at most 0.025.
Values may be sent and summed in bfloat16 or wider, within the bound.
No kernel may reach another device: no remote copies, remote signals or barrier semaphores. Data moves between devices by JAX's collectives and lax.ppermute only.
A program may use at most 192 MiB of HBM per device.

```python
import math
import jax
import jax.numpy as jnp
import numpy as np
from jax import lax

D = 3072
H = 24
HD = 128
FFW = 6144
BLOCK = 128
TOK_DEV = 1024
RMAX = 4
RAVG = 2
TOKENS = 16384
NBLK_DEV = 8
N_PATCH = 16


def draw_key_cache(key, part):
    key = jax.random.fold_in(key, 7)
    base_key = jax.random.fold_in(key, 0)
    drawn = jnp.clip(jax.random.normal(base_key, (TOKENS, H * HD), jnp.float32), -6.0, 6.0) * 3.0
    return drawn.astype(jnp.bfloat16)


def steps_of(rng, shape, cuts, least, top_value):
    def one(axis_at, parts):
        draws = jax.random.uniform(jax.random.fold_in(jax.random.fold_in(rng, 6), axis_at), (parts,), jnp.float32, least / len(cuts), top_value / len(cuts))
        return jnp.repeat(jnp.exp(draws), shape[axis_at] // parts).reshape((-1,) + (1,) * (len(shape) - axis_at - 1))

    factor_of = one(*cuts[0])
    for cut in cuts[1:]:
        factor_of = factor_of * one(*cut)
    return factor_of


def split_up(amount, total, most, lean):
    portions = [(1 << 20) // math.isqrt(standing ** lean) + 1 for standing in range(2, amount + 1)]
    spare, given = total - most - (amount - 1), [1] * (amount - 1)
    while spare > 0:
        candidates = [i for i in range(amount - 1) if given[i] < most]
        pool, left = sum([portions[i] for i in candidates]), spare
        for i in candidates:
            addition = min(most - given[i], max(1, left * portions[i] // pool), spare)
            given[i] = given[i] + addition
            spare = spare - addition
    return np.array([most] + given)


def ragged(key, number_of, total, most, slope):
    if number_of == 2:
        one = jax.random.randint(key, (), max(1, total - most), min(most, total - 1) + 1)
        return jnp.stack([one, total - one])
    sizes = jnp.asarray(split_up(number_of, total, most, slope), jnp.int32)
    pairs = (number_of - 1) // 2
    giver, taker = sizes[1:1 + 2 * pairs:2], sizes[2:2 + 2 * pairs:2]
    margin = jnp.minimum(giver - 1, most - taker)
    moved = jax.random.randint(jax.random.fold_in(key, 1), (pairs,), 0, 1 << 20) % (margin + 1)
    sizes = sizes.at[1:1 + 2 * pairs:2].set(giver - moved).at[2:2 + 2 * pairs:2].set(taker + moved)
    return sizes[jax.random.permutation(jax.random.fold_in(key, 2), number_of)]


def noise(own_key, shape, scale, reach, cuts=(), held_as=jnp.bfloat16):
    array = scale * jax.random.normal(own_key, shape, jnp.float32)
    if cuts:
        array = array * steps_of(own_key, shape, cuts, -0.22, 0.18)
    return jnp.clip(array, -reach, reach).astype(held_as)


def setup_inputs(seed: int = 0) -> dict:
    key_list = jax.random.split(jax.random.key(seed), 13)
    hidden = noise(key_list[0], (TOKENS, D), 1.0, 6.0, ((0, 16), (1, 8)))
    key_cache = draw_key_cache(jax.random.fold_in(key_list[12], 71), 0)
    value_cache = noise(key_list[2], (TOKENS, H * HD), 1.0, 6.0, ((0, 16), (1, 8)))
    block_order = jax.vmap(lambda own: jax.random.permutation(own, NBLK_DEV))(jax.random.split(key_list[3], N_PATCH)).reshape((N_PATCH, NBLK_DEV)).astype(jnp.int32)
    refresh_counts = ragged(key_list[4], N_PATCH, RAVG * N_PATCH, RMAX, 2).astype(jnp.int32)
    modulation = noise(key_list[5], (3, D), 1.0, 4.0, (), jnp.float32)
    query_gain = jnp.clip(1.0 + 0.15 * jax.random.normal(key_list[6], (HD,), jnp.float32), 0.25, 1.75)
    key_gain = jnp.clip(jnp.exp(jax.random.uniform(key_list[7], (HD,), jnp.float32, math.log(2.0), math.log(4.0))), 2.0, 4.0)
    w_qkv = noise(key_list[8], (D, 3, H * HD), D ** -0.5, 0.109375, ((2, 8),))
    w_mlp = noise(key_list[9], (D, FFW), D ** -0.5, 0.109375, ((1, 8),))
    w_out_attn = noise(key_list[10], (H * HD, D), (H * HD + FFW) ** -0.5, 0.0625, ((0, 8),))
    w_out_mlp = noise(key_list[11], (FFW, D), (H * HD + FFW) ** -0.5, 0.0625, ((0, 8),))
    return dict(hidden=hidden, key_cache=key_cache, value_cache=value_cache, block_order=block_order, refresh_counts=refresh_counts, modulation=modulation, query_gain=query_gain, key_gain=key_gain, w_qkv=w_qkv, w_mlp=w_mlp, w_out_attn=w_out_attn, w_out_mlp=w_out_mlp)


def layer_norm_mod(token_rows, modulation):
    values = token_rows.astype(jnp.float32)
    center = values - lax.optimization_barrier(jnp.mean(values, axis=-1, keepdims=True))
    spread = lax.optimization_barrier(jnp.mean(center * center, axis=-1, keepdims=True))
    normed = center * lax.rsqrt(spread + 1e-06)
    return (normed * (1.0 + modulation[1]) + modulation[0]).astype(jnp.bfloat16)

def rms_scale(values, gain):
    scaled = values * lax.rsqrt(lax.optimization_barrier(jnp.mean(values * values, axis=-1, keepdims=True)) + 1e-06) * gain
    return scaled.astype(jnp.bfloat16)

def reference(hidden, key_cache, value_cache, block_order, refresh_counts, modulation, query_gain, key_gain, w_qkv, w_mlp, w_out_attn, w_out_mlp):
    num_blocks = TOK_DEV // BLOCK
    head_cols = H * HD
    live_count = RAVG * N_PATCH
    slot_index = jnp.arange(N_PATCH * RMAX, dtype=jnp.int32)
    shard_of = (slot_index // RMAX).astype(jnp.int32)
    within = (slot_index % RMAX).astype(jnp.int32)
    slot_on = within < refresh_counts[shard_of]
    live_slots = jnp.nonzero(slot_on, size=live_count)[0].astype(jnp.int32)
    global_block = (shard_of * num_blocks + block_order[shard_of, within]).astype(jnp.int32)
    live_blocks = global_block[live_slots].astype(jnp.int32)
    token_rows = hidden.reshape(-1, BLOCK, D)[live_blocks].reshape(-1, D)
    modded = layer_norm_mod(token_rows, modulation)
    projected = jnp.dot(modded, w_qkv.reshape(D, 3 * head_cols), preferred_element_type=jnp.float32)
    query_new = rms_scale(projected[:, :head_cols].reshape(-1, H, HD), query_gain)
    key_new = rms_scale(projected[:, head_cols:2 * head_cols].reshape(-1, H, HD), key_gain)
    value_new = projected[:, 2 * head_cols:].astype(jnp.bfloat16)
    mlp_hidden = jax.nn.gelu(jnp.dot(modded, w_mlp, preferred_element_type=jnp.float32), approximate=True).astype(jnp.bfloat16)
    key_all = key_cache.reshape(-1, BLOCK, head_cols).at[live_blocks].set(key_new.reshape(-1, BLOCK, head_cols))
    value_all = value_cache.reshape(-1, BLOCK, head_cols).at[live_blocks].set(value_new.reshape(-1, BLOCK, head_cols))
    key_float = key_all.reshape(-1, H, HD).astype(jnp.float32)
    value_float = value_all.reshape(-1, H, HD).astype(jnp.float32)
    group_rows = math.gcd(live_count * BLOCK, 256)
    query_blocks = query_new.reshape(-1, group_rows, H, HD)

    def attend(query_group):
        scores = jnp.einsum('qhd,khd->hqk', query_group.astype(jnp.float32), key_float) * HD ** (-0.5)
        row_top = lax.optimization_barrier(jnp.max(scores, axis=-1, keepdims=True))
        weights = jnp.exp(scores - row_top)
        row_total = lax.optimization_barrier(jnp.sum(weights, axis=-1))
        rounded = lax.optimization_barrier(weights.astype(jnp.bfloat16))
        numerator = jnp.einsum('hqk,khd->qhd', rounded.astype(jnp.float32), value_float)
        return (numerator / jnp.transpose(row_total)[:, :, None]).astype(jnp.bfloat16)
    attention = lax.map(attend, query_blocks).reshape(-1, head_cols)
    branch_sum = jnp.dot(attention, w_out_attn, preferred_element_type=jnp.float32) + jnp.dot(mlp_hidden, w_out_mlp, preferred_element_type=jnp.float32)
    result = (token_rows.astype(jnp.float32) + modulation[2] * branch_sum).astype(jnp.bfloat16)
    output = jnp.zeros((N_PATCH * RMAX, BLOCK, D), jnp.bfloat16).at[live_slots].set(result.reshape(-1, BLOCK, D))
    return output.reshape(-1, D)
```

```python
import functools
import math

import jax
import jax.numpy as jnp
from jax import lax
from jax.experimental import pallas as pl
from jax.experimental.pallas import tpu as pltpu
from jax.sharding import PartitionSpec as P

HD = 128
BLOCK = 128
RMAX = 4
NZ = 4
SIDE = 4
LSE_ROWS = 16
BF16 = jnp.bfloat16
F32 = jnp.float32
EXP2_SCALE = HD ** (-0.5) * math.log2(math.e)
VMEM = pltpu.VMEM


def whole(shape):
    return pl.BlockSpec(shape, lambda *_: (0,) * len(shape), memory_space=VMEM)


def params(mib):
    return pltpu.CompilerParams(vmem_limit_bytes=mib * 2**20)


def pick_rows_kernel(order, hidden_ref, rows_ref):
    rows_ref[...] = hidden_ref[...]


def pick_rows(order, hidden):
    width = hidden.shape[1]
    return pl.pallas_call(
        pick_rows_kernel,
        grid_spec=pltpu.PrefetchScalarGridSpec(
            num_scalar_prefetch=1,
            grid=(RMAX,),
            in_specs=[pl.BlockSpec((BLOCK, width), lambda i, order: (order[i], 0))],
            out_specs=pl.BlockSpec((BLOCK, width), lambda i, order: (i, 0)),
        ),
        out_shape=jax.ShapeDtypeStruct((RMAX * BLOCK, width), BF16),
        compiler_params=params(16),
        name="pick_rows",
    )(order, hidden)


def pick_cache_kernel(order, key_slot, value_slot, key_rest, value_rest, slots_ref, rest_ref):
    width = key_slot.shape[1]
    slots_ref[:, :width] = key_slot[...]
    slots_ref[:, width:] = value_slot[...]
    rest_ref[:, :width] = key_rest[...]
    rest_ref[:, width:] = value_rest[...]


def pick_cache(order, key_cache, value_cache):
    width = key_cache.shape[1]
    slot = pl.BlockSpec((BLOCK, width), lambda i, order: (order[i], 0))
    rest = pl.BlockSpec((BLOCK, width), lambda i, order: (order[RMAX + i], 0))
    out = pl.BlockSpec((BLOCK, 2 * width), lambda i, order: (i, 0))
    shape = jax.ShapeDtypeStruct((RMAX * BLOCK, 2 * width), BF16)
    return pl.pallas_call(
        pick_cache_kernel,
        grid_spec=pltpu.PrefetchScalarGridSpec(
            num_scalar_prefetch=1,
            grid=(RMAX,),
            in_specs=[slot, slot, rest, rest],
            out_specs=[out, out],
        ),
        out_shape=[shape, shape],
        compiler_params=params(16),
        name="pick_cache",
    )(order, key_cache, value_cache, key_cache, value_cache)


def project_kernel(
    place, r0, r1, r2, r3, s0, s1, s2, s3, mod_ref, qg_ref, kg_ref, w_ref, old_ref,
    q_ref, kv_ref, modded_ref,
):
    step = pl.program_id(0)
    z, core, count = place[0], place[1], place[2]
    pieces = []
    for k in range(NZ):
        zs = lax.rem(z - k + NZ, NZ)
        pieces.append(((r0, r1, r2, r3)[k], zs * 2 + core))
        pieces.append(((s0, s1, s2, s3)[k], zs * 2 + 1 - core))
    rows, width = r0.shape
    features = width * len(pieces)
    tall = 64

    @pl.when(step == 0)
    def _():
        def norm(i, carry):
            here = pl.ds(pl.multiple_of(i * tall, tall), tall)
            total = jnp.zeros((tall, width), F32)
            for ref, _h in pieces:
                total = total + ref[here, :].astype(F32)
            mean = jnp.sum(total, axis=-1, keepdims=True) * (1.0 / features)
            square = jnp.zeros((tall, width), F32)
            for ref, _h in pieces:
                center = ref[here, :].astype(F32) - mean
                square = square + center * center
            spread = jnp.sum(square, axis=-1, keepdims=True) * (1.0 / features)
            inv = lax.rsqrt(spread + 1e-06)
            for ref, h in pieces:
                cols = pl.ds(pl.multiple_of(h * width, 128), width)
                normed = (ref[here, :].astype(F32) - mean) * inv
                out = normed * (1.0 + mod_ref[1:2, cols]) + mod_ref[0:1, cols]
                modded_ref[here, cols] = out.astype(BF16)
            return carry

        lax.fori_loop(0, rows // tall, norm, 0)

    def half(i, carry):
        here = pl.ds(pl.multiple_of(i * 256, 256), 256)
        acc = jnp.dot(modded_ref[here, :], w_ref[...], preferred_element_type=F32)

        def rms(gain):
            out = []
            for j in range(width // HD):
                v = acc[:, j * HD : (j + 1) * HD]
                scale = lax.rsqrt(jnp.mean(v * v, axis=-1, keepdims=True) + 1e-06)
                out.append((v * scale * gain).astype(BF16))
            return jnp.concatenate(out, axis=1)

        first = i * 256
        fresh = first + lax.broadcasted_iota(jnp.int32, (256, width), 0) < count * BLOCK

        @pl.when(step == 0)
        def _():
            q_ref[here, :] = rms(qg_ref[...])

        @pl.when(step == 1)
        def _():
            old = old_ref[here, :width]
            kv_ref[here, :width] = jnp.where(fresh, rms(kg_ref[...]).astype(F32), old.astype(F32)).astype(BF16)

        @pl.when(step == 2)
        def _():
            old = old_ref[here, width:]
            kv_ref[here, width:] = jnp.where(fresh, acc, old.astype(F32)).astype(BF16)

        return carry

    lax.fori_loop(0, rows // 256, half, 0)


def project(place, own, swapped, modulation, query_gain, key_gain, w_qkv, old):
    rows, width = own[0].shape
    features = w_qkv.shape[0]
    return pl.pallas_call(
        project_kernel,
        grid_spec=pltpu.PrefetchScalarGridSpec(
            num_scalar_prefetch=1,
            grid=(3,),
            in_specs=[whole((rows, width))] * 8
            + [whole(modulation.shape), whole((1, HD)), whole((1, HD))]
            + [pl.BlockSpec((features, width), lambda i, *_: (0, i)), whole(old.shape)],
            out_specs=[whole((rows, width)), whole((rows, 2 * width)), whole((rows, features))],
        ),
        out_shape=[
            jax.ShapeDtypeStruct((rows, width), BF16),
            jax.ShapeDtypeStruct((rows, 2 * width), BF16),
            jax.ShapeDtypeStruct((rows, features), BF16),
        ],
        compiler_params=params(48),
        cost_estimate=pl.CostEstimate(
            flops=2 * rows * features * 3 * width, bytes_accessed=14_000_000, transcendentals=0
        ),
        name="project",
    )(place, *own, *swapped, modulation, query_gain.reshape(1, HD), key_gain.reshape(1, HD), w_qkv, old)


def mlp_kernel(modded_ref, w_ref, out_ref):
    def half(i, carry):
        here = pl.ds(pl.multiple_of(i * 256, 256), 256)
        acc = jnp.dot(modded_ref[here, :], w_ref[...], preferred_element_type=F32)
        out_ref[here, :] = jax.nn.gelu(acc, approximate=True).astype(BF16)
        return carry

    lax.fori_loop(0, modded_ref.shape[0] // 256, half, 0)


def mlp_in(modded, w_mlp):
    rows, features = modded.shape
    hidden = w_mlp.shape[1]
    tile = 256
    return pl.pallas_call(
        mlp_kernel,
        grid=(hidden // tile,),
        in_specs=[whole(modded.shape), pl.BlockSpec((features, tile), lambda i: (0, i))],
        out_specs=pl.BlockSpec((rows, tile), lambda i: (0, i)),
        out_shape=jax.ShapeDtypeStruct((rows, hidden), BF16),
        compiler_params=params(40),
        cost_estimate=pl.CostEstimate(
            flops=2 * rows * features * hidden, bytes_accessed=9_000_000, transcendentals=0
        ),
        name="mlp_in",
    )(modded, w_mlp)


def attend_kernel(counts, *refs):
    q_refs, k_refs, v_refs = refs[:4], refs[4:12], refs[12:20]
    o_refs, (qs, os_, ls) = refs[20:24], refs[24:]
    rows = q_refs[0].shape[0]
    slots = rows // BLOCK
    starts, total = [], 0
    for s in range(SIDE):
        starts.append(total)
        total = total + counts[s]

    for s in range(SIDE):
        for i in range(slots):
            @pl.when(i < counts[s])
            def _(s=s, i=i):
                to = pl.ds(pl.multiple_of((starts[s] + i) * BLOCK, BLOCK), BLOCK)
                qs[to, :] = q_refs[s][i * BLOCK : (i + 1) * BLOCK, :]

    def tile(t, carry):
        here = pl.ds(pl.multiple_of(t * 2 * BLOCK, 2 * BLOCK), 2 * BLOCK)
        q = qs[here, :]
        scores = [
            lax.dot_general(q, k[...], (((1,), (1,)), ((), ())), preferred_element_type=F32)
            for k in k_refs
        ]
        top = functools.reduce(jnp.maximum, scores)
        top = jnp.max(top, axis=-1, keepdims=True)
        acc = jnp.zeros((2 * BLOCK, 2 * HD), F32)
        ones = jnp.ones((rows, HD), BF16)
        for score, v in zip(scores, v_refs):
            weights = jnp.exp2((score - top) * EXP2_SCALE).astype(BF16)
            acc = acc + jnp.dot(
                weights, jnp.concatenate([v[...], ones], axis=1), preferred_element_type=F32
            )
        os_[here, :] = (acc[:, :HD] / acc[:, HD:]).astype(BF16)
        ls[here, :] = top * EXP2_SCALE + jnp.log2(acc[:, HD:])
        return carry

    lax.fori_loop(0, lax.div(total + 1, 2), tile, 0)

    line = lax.broadcasted_iota(jnp.int32, (LSE_ROWS, BLOCK), 0)
    for s in range(SIDE):
        packed = jnp.zeros((LSE_ROWS, BLOCK), F32)
        for i in range(slots):
            at = jnp.where(i < counts[s], starts[s] + i, 0)
            here = pl.ds(pl.multiple_of(at * BLOCK, BLOCK), BLOCK)
            o_refs[s][i * BLOCK : (i + 1) * BLOCK, :] = os_[here, :]
            lse = jnp.transpose(ls[here, :])[:LSE_ROWS, :]
            high = lse.astype(BF16).astype(F32)
            mid = (lse - high).astype(BF16).astype(F32)
            low = lse - high - mid
            part = line - 4 * i
            packed = jnp.where(part == 0, high, packed)
            packed = jnp.where(part == 1, mid, packed)
            packed = jnp.where(part == 2, low, packed)
        o_refs[s][rows : rows + LSE_ROWS, :] = packed.astype(BF16)


def attend(counts, queries, caches):
    rows, width = queries[0].shape
    heads = width // HD
    key_block = pl.BlockSpec((rows, HD), lambda j, *_: (0, j))
    value_block = pl.BlockSpec((rows, HD), lambda j, *_: (0, heads + j))
    tall = rows + LSE_ROWS
    return pl.pallas_call(
        attend_kernel,
        grid_spec=pltpu.PrefetchScalarGridSpec(
            num_scalar_prefetch=1,
            grid=(heads,),
            in_specs=[key_block] * 4 + [key_block] * 8 + [value_block] * 8,
            out_specs=[pl.BlockSpec((tall, HD), lambda j, *_: (0, j))] * 4,
            scratch_shapes=[
                VMEM((SIDE * rows, HD), BF16),
                VMEM((SIDE * rows, HD), BF16),
                VMEM((SIDE * rows, HD), F32),
            ],
        ),
        out_shape=[jax.ShapeDtypeStruct((tall, width), BF16)] * 4,
        compiler_params=params(48),
        cost_estimate=pl.CostEstimate(
            flops=12_000_000_000, bytes_accessed=10_000_000, transcendentals=12_000_000
        ),
        name="attend",
    )(counts, *queries, *caches, *caches)


def branch_send_kernel(cols, p0, p1, p2, p3, mlp_ref, wa_ref, wm_ref, send_ref, attn_ref):
    parts = (p0, p1, p2, p3)
    rows = mlp_ref.shape[0]
    heads = attn_ref.shape[1] // HD

    @pl.when(pl.program_id(0) == 0)
    def _():
        for j in range(heads):
            lanes = slice(j * HD, (j + 1) * HD)
            lses = [p[rows : rows + LSE_ROWS, lanes].astype(F32) for p in parts]
            for i in range(rows // BLOCK):
                each = []
                for lse in lses:
                    total = lse[4 * i : 4 * i + 1] + lse[4 * i + 1 : 4 * i + 2] + lse[4 * i + 2 : 4 * i + 3]
                    each.append(jnp.broadcast_to(total, (BLOCK, BLOCK)))
                top = functools.reduce(jnp.maximum, each)
                shares = [jnp.exp2(e - top) for e in each]
                scale = 1.0 / functools.reduce(jnp.add, shares)
                here = slice(i * BLOCK, (i + 1) * BLOCK)
                mixed = jnp.zeros((BLOCK, HD), F32)
                for share, p in zip(shares, parts):
                    mixed = mixed + jnp.transpose(share * scale) * p[here, lanes].astype(F32)
                attn_ref[here, lanes] = mixed.astype(BF16)

    acc = jnp.dot(attn_ref[...], wa_ref[...], preferred_element_type=F32)
    acc = acc + jnp.dot(mlp_ref[...], wm_ref[...], preferred_element_type=F32)
    send_ref[0] = acc.astype(BF16)


def branch_keep_kernel(cols, attn_ref, mlp_ref, wa_ref, wm_ref, keep_ref):
    acc = jnp.dot(attn_ref[...], wa_ref[...], preferred_element_type=F32)
    acc = acc + jnp.dot(mlp_ref[...], wm_ref[...], preferred_element_type=F32)
    keep_ref[0] = acc.astype(BF16)


def branch(cols, inputs, mlp_hidden, w_attn, w_mlp, first):
    rows = mlp_hidden.shape[0]
    width = w_attn.shape[0]
    specs = [whole(a.shape) for a in inputs] + [
        whole(mlp_hidden.shape),
        pl.BlockSpec((w_attn.shape[0], width), lambda i, cols: (0, cols[i])),
        pl.BlockSpec((w_mlp.shape[0], width), lambda i, cols: (0, cols[i])),
    ]
    out_specs = [pl.BlockSpec((1, rows, width), lambda i, cols: (i, 0, 0))]
    out_shape = [jax.ShapeDtypeStruct((NZ, rows, width), BF16)]
    if first:
        out_specs.append(whole((rows, width)))
        out_shape.append(jax.ShapeDtypeStruct((rows, width), BF16))
    return pl.pallas_call(
        branch_send_kernel if first else branch_keep_kernel,
        grid_spec=pltpu.PrefetchScalarGridSpec(
            num_scalar_prefetch=1, grid=(NZ,), in_specs=specs, out_specs=out_specs
        ),
        out_shape=out_shape,
        compiler_params=params(40),
        cost_estimate=pl.CostEstimate(
            flops=2 * rows * (width + w_mlp.shape[0]) * NZ * width,
            bytes_accessed=7_000_000,
            transcendentals=0,
        ),
        name="branch_send" if first else "branch_keep",
    )(cols, *inputs, mlp_hidden, w_attn, w_mlp)


def along_x(a, k):
    return lax.ppermute(a, "patch", [(y * 4 + x, y * 4 + (x + k) % 4) for y in range(4) for x in range(4)])


def along_y(a, k):
    return lax.ppermute(a, "patch", [(y * 4 + x, (y + k) % 4 * 4 + x) for y in range(4) for x in range(4)])


def along_z(a, k):
    return lax.ppermute(a, "head", [(z * 2 + c, (z + k) % 4 * 2 + c) for z in range(4) for c in range(2)])


def other_core(a):
    return lax.ppermute(a, "head", [(i, i ^ 1) for i in range(8)])


def body(
    hidden, key_cache, value_cache, block_order, refresh_counts, modulation,
    query_gain, key_gain, w_qkv, w_mlp, w_out_attn, w_out_mlp,
):
    width = hidden.shape[1]
    order = block_order[0]
    count = refresh_counts[0]
    head = lax.axis_index("head")
    z, core = head // 2, head % 2

    rows = pick_rows(order, hidden)
    far = {k: along_z(rows, k) for k in (1, 3, 2)}
    own = [rows, far[1], far[2], far[3]]
    swapped = [other_core(a) for a in own]

    old_slots, rest = pick_cache(order, key_cache, value_cache)
    rest_far = {k: along_y(rest, k) for k in (1, 3, 2)}
    counts_far = {k: along_x(refresh_counts, k) for k in (1, 3, 2)}
    counts = jnp.concatenate([refresh_counts, counts_far[1], counts_far[2], counts_far[3]])

    place = jnp.stack([z, core, count]).astype(jnp.int32)
    queries, fresh, modded = project(
        place, own, swapped, modulation, query_gain, key_gain,
        w_qkv.reshape(w_qkv.shape[0], 3 * width), old_slots,
    )
    query_far = {k: along_x(queries, k) for k in (1, 3, 2)}
    fresh_far = {k: along_y(fresh, k) for k in (1, 3, 2)}
    mlp_hidden = mlp_in(modded, w_mlp)

    parts = attend(
        counts,
        [queries, query_far[1], query_far[2], query_far[3]],
        [rest, rest_far[1], rest_far[2], rest_far[3], fresh, fresh_far[1], fresh_far[2], fresh_far[3]],
    )
    back = {k: along_x(parts[k], -k) for k in (1, 3, 2)}

    ahead = (z + jnp.arange(NZ)) % NZ * 2
    send, attn = branch(
        (ahead + 1 - core).astype(jnp.int32),
        [parts[0], back[1], back[2], back[3]], mlp_hidden, w_out_attn, w_out_mlp, True,
    )
    (keep,) = branch((ahead + core).astype(jnp.int32), [attn], mlp_hidden, w_out_attn, w_out_mlp, False)
    got = other_core(send)
    chip = keep.astype(F32) + got.astype(F32)
    summed = chip[0]
    for k in (2, 1, 3):
        summed = summed + along_z(chip[k].astype(BF16), k).astype(F32)

    gate = lax.dynamic_slice_in_dim(modulation[2], head * width, width)
    result = (rows.astype(F32) + gate * summed).astype(BF16)
    live = jnp.arange(rows.shape[0]) < count * BLOCK
    return jnp.where(live[:, None], result, jnp.zeros((), BF16))


def solution(mesh):
    in_specs = (
        P("patch", "head"), P("patch", "head"), P("patch", "head"), P("patch", None), P("patch"),
        P(), P(), P(),
        P(None, None, "head"), P(None, "head"), P("head", None), P("head", None),
    )
    return jax.shard_map(
        body, mesh=mesh, in_specs=in_specs, out_specs=P("patch", "head"), check_vma=False
    )
```

```python
import functools
import math

import jax
import jax.numpy as jnp
from jax import lax
from jax.experimental import pallas as pl
from jax.experimental.pallas import tpu as pltpu
from jax.sharding import PartitionSpec as P

HD = 128
BLOCK = 128
RMAX = 4
NZ = 4
SIDE = 4
LSE_ROWS = 16
NOTE_ROWS = 16
PER_US = 1_100_000_000
BF16 = jnp.bfloat16
F32 = jnp.float32
EXP2_SCALE = HD ** (-0.5) * math.log2(math.e)
VMEM = pltpu.VMEM


def spec(space):
    return pl.BlockSpec(memory_space=space)


def in_vmem(a):
    return pltpu.with_memory_space_constraint(a, VMEM)


def in_hbm(a):
    return pltpu.with_memory_space_constraint(a, pltpu.HBM)


def call(kernel, operands, outs, scalars=None, far=(), scratch=(), mib=16, cost=0, name=None):
    specs = [spec(VMEM)] * len(operands) + [spec(pltpu.HBM)] * len(far)
    operands = [in_vmem(a) for a in operands] + [in_hbm(a) for a in far]
    if scalars is not None:
        specs = [spec(pltpu.SMEM)] + specs
        operands = [scalars] + operands
    return pl.pallas_call(
        kernel,
        in_specs=specs,
        out_specs=[spec(VMEM)] * len(outs),
        out_shape=[VMEM(shape, dtype) for shape, dtype in outs],
        scratch_shapes=list(scratch),
        compiler_params=pltpu.CompilerParams(vmem_limit_bytes=mib * 2**20),
        cost_estimate=pl.CostEstimate(flops=cost, bytes_accessed=1000, transcendentals=0),
        name=name,
    )(*operands)


def copies_of(pairs, sems):
    copies = [pltpu.make_async_copy(src, dst, sems.at[n]) for n, (src, dst) in enumerate(pairs)]
    for copy in copies:
        copy.start()
    return copies


def block_at(order, place):
    return pl.ds(pl.multiple_of(order[0, place] * BLOCK, BLOCK), BLOCK)


def pick_rows_kernel(order, hidden, out, sems):
    pairs = [
        (hidden.at[block_at(order, i), :], out.at[pl.ds(i * BLOCK, BLOCK), :]) for i in range(RMAX)
    ]
    for copy in copies_of(pairs, sems):
        copy.wait()


def pick_rows(order, hidden):
    return call(
        pick_rows_kernel, [], [((RMAX * BLOCK, hidden.shape[1]), BF16)], scalars=order, far=[hidden],
        scratch=[pltpu.SemaphoreType.DMA((RMAX,))], name="pick_rows",
    )


def pick_cache_kernel(order, keys, values, rest_ref, old_ref, sems):
    pairs = []
    width = keys.shape[1]
    for i in range(2 * RMAX):
        here, to = block_at(order, (RMAX + i) % (2 * RMAX)), pl.ds(i % RMAX * BLOCK, BLOCK)
        for n, ref in enumerate((keys, values)):
            out = rest_ref if i < RMAX else old_ref
            pairs.append((ref.at[here, :], out.at[to, pl.ds(n * width, width)]))
    for copy in copies_of(pairs, sems):
        copy.wait()


def pick_cache(order, keys, values):
    return call(
        pick_cache_kernel, [], [((RMAX * BLOCK, 2 * keys.shape[1]), BF16)] * 2, scalars=order,
        far=[keys, values], scratch=[pltpu.SemaphoreType.DMA((4 * RMAX,))], name="pick_cache",
    )


def project_kernel(
    place, p0, p1, p2, p3, p4, p5, p6, p7, mod_ref, qg_ref, kg_ref, old_ref, w_ref,
    q_ref, kv_ref, modded_ref, w_vmem, sems,
):
    pieces = (p0, p1, p2, p3, p4, p5, p6, p7)
    z, core, count = place[0], place[1], place[2]
    rows, width = p0.shape
    features = width * len(pieces)
    weight_copies = copies_of([(w_ref.at[n], w_vmem.at[n]) for n in range(3)], sems)
    near = lax.rem(z + NZ - 1 + 2 * core, NZ)
    away = lax.rem(z + NZ + 1 - 2 * core, NZ)
    across = lax.rem(z + 2, NZ)
    homes = [
        zone * 2 + side
        for zone, side in (
            (z, core), (z, 1 - core), (near, core), (near, 1 - core),
            (across, core), (away, 1 - core), (away, core), (across, 1 - core),
        )
    ]
    tall = 32

    def norm(i, carry):
        here = pl.ds(pl.multiple_of(i * tall, tall), tall)
        total = jnp.zeros((tall, width), F32)
        for n in range(8):
            total = total + pieces[n][here, :].astype(F32)
        mean = jnp.sum(total, axis=-1, keepdims=True) * (1.0 / features)
        square = jnp.zeros((tall, width), F32)
        for n in range(8):
            center = pieces[n][here, :].astype(F32) - mean
            square = square + center * center
        spread = jnp.sum(square, axis=-1, keepdims=True) * (1.0 / features)
        inv = lax.rsqrt(spread + 1e-06)
        for n, h in enumerate(homes):
            cols = pl.ds(pl.multiple_of(h * width, 128), width)
            normed = (pieces[n][here, :].astype(F32) - mean) * inv
            out = normed * (1.0 + mod_ref[1:2, cols]) + mod_ref[0:1, cols]
            modded_ref[here, cols] = out.astype(BF16)
        return carry

    lax.fori_loop(0, rows // tall, norm, 0, unroll=2)

    def rms(acc, gain):
        out = []
        for j in range(width // HD):
            v = acc[:, j * HD : (j + 1) * HD]
            scale = lax.rsqrt(jnp.mean(v * v, axis=-1, keepdims=True) + 1e-06)
            out.append(v * scale * gain)
        return jnp.concatenate(out, axis=1)

    slices = [slice(i * 256, (i + 1) * 256) for i in range(rows // 256)]
    fresh = [
        i * 256 + lax.broadcasted_iota(jnp.int32, (256, width), 0) < count * BLOCK
        for i in range(rows // 256)
    ]

    def dot(here, n):
        return jnp.dot(modded_ref[here, :], w_vmem[n], preferred_element_type=F32)

    weight_copies[0].wait()
    for here in slices:
        q_ref[here, :] = rms(dot(here, 0), qg_ref[...]).astype(BF16)
    q_ref[rows : rows + NOTE_ROWS, :] = (
        jnp.full((NOTE_ROWS, width), count, jnp.int32).astype(F32).astype(BF16)
    )
    weight_copies[1].wait()
    for here, live in zip(slices, fresh):
        key = rms(dot(here, 1), kg_ref[...])
        kv_ref[here, :width] = jnp.where(live, key, old_ref[here, :width].astype(F32)).astype(BF16)
    weight_copies[2].wait()
    for here, live in zip(slices, fresh):
        value = dot(here, 2)
        kv_ref[here, width:] = jnp.where(live, value, old_ref[here, width:].astype(F32)).astype(BF16)


def project(place, pieces, modulation, query_gain, key_gain, w_qkv, old):
    rows, width = pieces[0].shape
    features = w_qkv.shape[1]
    return call(
        project_kernel,
        [*pieces, modulation, query_gain.reshape(1, HD), key_gain.reshape(1, HD), old],
        [((rows + NOTE_ROWS, width), BF16), ((rows, 2 * width), BF16), ((rows, features), BF16)],
        scalars=place, far=[w_qkv],
        scratch=[VMEM(w_qkv.shape, BF16), pltpu.SemaphoreType.DMA((3,))], cost=10 * PER_US, name="project",
    )


def mlp_kernel(modded_ref, w_ref, out_ref, w_vmem, sems):
    width = w_ref.shape[1] // 3
    tiles = [slice(j * width, (j + 1) * width) for j in range(3)]
    copies = copies_of(
        [(w_ref.at[:, pl.ds(j * width, width)], w_vmem.at[j]) for j in range(3)], sems
    )
    for j in range(3):
        copies[j].wait()
        for i in range(modded_ref.shape[0] // 256):
            here = slice(i * 256, (i + 1) * 256)
            acc = jnp.dot(modded_ref[here, :], w_vmem[j], preferred_element_type=F32)
            out_ref[here, tiles[j]] = jax.nn.gelu(acc, approximate=True).astype(BF16)


def mlp_in(modded, w_mlp):
    rows, features = modded.shape
    hidden = w_mlp.shape[1]
    return call(
        mlp_kernel, [modded], [((rows, hidden), BF16)], far=[w_mlp],
        scratch=[VMEM((3, features, hidden // 3), BF16), pltpu.SemaphoreType.DMA((3,))],
        cost=5 * PER_US, name="mlp_in",
    )[0]


def attend_kernel(*refs, n_keys, chained, last):
    refs = list(refs)

    def take(n):
        out = refs[:n]
        del refs[:n]
        return out

    q_refs, kv_refs = take(SIDE), take(n_keys)
    o_in, lse_in = take(2) if chained else (None, None)
    out_refs = take(SIDE) if last else None
    o_out, lse_out, qs = take(3)
    rows, width = q_refs[0].shape[0] - NOTE_ROWS, q_refs[0].shape[1]
    slots, heads = rows // BLOCK, width // HD

    starts, live, total = [], [], 0
    for s in range(SIDE):
        count = jnp.max(q_refs[s][rows : rows + NOTE_ROWS, :HD].astype(F32)).astype(jnp.int32)
        starts.append(total)
        live.append(count)
        total = total + count

    for s in range(SIDE):
        for i in range(slots):
            @pl.when(i < live[s])
            def _(s=s, i=i):
                to = pl.ds(pl.multiple_of((starts[s] + i) * BLOCK, BLOCK), BLOCK)
                qs[to, :] = q_refs[s][i * BLOCK : (i + 1) * BLOCK, :]

    def lanes(j):
        return slice(j * HD, (j + 1) * HD)

    def tile(t, carry):
        here = pl.ds(pl.multiple_of(t * 2 * BLOCK, 2 * BLOCK), 2 * BLOCK)

        def score(j):
            q = qs[here, lanes(j)]
            return [
                lax.dot_general(q, kv[:, lanes(j)], (((1,), (1,)), ((), ())), preferred_element_type=F32)
                for kv in kv_refs
            ]

        ahead = score(0)
        for j in range(heads):
            scores = ahead
            if j + 1 < heads:
                ahead = score(j + 1)
            top = functools.reduce(jnp.maximum, [jnp.max(s, axis=-1, keepdims=True) for s in scores])
            top = top * EXP2_SCALE
            if chained:
                lse = lse_in[here, lanes(j)]
                top = jnp.maximum(top, lse[:, :1])
                share = jnp.exp2(lse - top)
                acc = jnp.concatenate([o_in[here, lanes(j)] * share, share], axis=1)
            else:
                acc = jnp.zeros((2 * BLOCK, 2 * HD), F32)
            for s, kv in zip(scores, kv_refs):
                weights = jnp.exp2(s * EXP2_SCALE - top).astype(BF16)
                value = kv[:, width + j * HD : width + (j + 1) * HD]
                value = jnp.concatenate([value, jnp.ones(value.shape, BF16)], axis=1)
                acc = acc + jnp.dot(weights, value, preferred_element_type=F32)
            o_out[here, lanes(j)] = acc[:, :HD] / acc[:, HD:]
            lse_out[here, lanes(j)] = top + jnp.log2(acc[:, HD:])
        return carry

    lax.fori_loop(0, lax.div(total + 1, 2), tile, 0)
    if not last:
        return

    line = lax.broadcasted_iota(jnp.int32, (LSE_ROWS, BLOCK), 0)
    for s in range(SIDE):
        out_refs[s][rows : rows + LSE_ROWS, :] = jnp.zeros((LSE_ROWS, width), BF16)
        for i in range(slots):
            @pl.when(i < live[s])
            def _(s=s, i=i):
                here = pl.ds(pl.multiple_of((starts[s] + i) * BLOCK, BLOCK), BLOCK)
                out_refs[s][i * BLOCK : (i + 1) * BLOCK, :] = o_out[here, :].astype(BF16)
                for j in range(heads):
                    lse = jnp.transpose(lse_out[here, lanes(j)])[:LSE_ROWS, :]
                    high = lse.astype(BF16).astype(F32)
                    mid = (lse - high).astype(BF16).astype(F32)
                    low = lse - high - mid
                    packed = out_refs[s][rows : rows + LSE_ROWS, lanes(j)].astype(F32)
                    part = line - 4 * i
                    packed = jnp.where(part == 0, high, packed)
                    packed = jnp.where(part == 1, mid, packed)
                    packed = jnp.where(part == 2, low, packed)
                    out_refs[s][rows : rows + LSE_ROWS, lanes(j)] = packed.astype(BF16)


def attend(queries, caches, state, last):
    tall, width = queries[0].shape
    rows = tall - NOTE_ROWS
    states = [((SIDE * rows, width), F32)] * 2
    scratch = [VMEM((SIDE * rows, width), BF16)]
    if last:
        outs = [((rows + LSE_ROWS, width), BF16)] * SIDE
        scratch = [VMEM(shape, dtype) for shape, dtype in states] + scratch
    else:
        outs = states
    return call(
        functools.partial(attend_kernel, n_keys=len(caches), chained=bool(state), last=last),
        [*queries, *caches, *state], outs, scratch=scratch, mib=20, cost=9 * PER_US,
        name="attend_last" if last else "attend_first",
    )


def columns(place, n, width):
    z, core = place[0], place[1]
    side = 1 - core if n < NZ else core
    h = lax.rem(z + n % NZ, NZ) * 2 + side
    return pl.ds(pl.multiple_of(h * width, 128), width)


def mlp_out_kernel(place, mlp_ref, w_ref, out_ref):
    for n in range(2 * NZ):
        cols = columns(place, n, out_ref.shape[2])
        out_ref[n] = jnp.dot(mlp_ref[...], w_ref[:, cols], preferred_element_type=F32)


def mlp_out(place, mlp_hidden, w_out):
    rows, hidden = mlp_hidden.shape
    width = w_out.shape[1] // (2 * NZ)
    return call(
        mlp_out_kernel, [mlp_hidden, w_out], [((2 * NZ, rows, width), F32)], scalars=place,
        cost=4 * PER_US, name="mlp_out",
    )[0]


def branch_kernel(place, *refs):
    parts, mlp_ref, w_ref = refs[:4], refs[4], refs[5]
    send_ref, keep_ref, attn_ref = refs[6:]
    rows, width = attn_ref.shape
    for j in range(width // HD):
        cols = slice(j * HD, (j + 1) * HD)
        lses = [p[rows : rows + LSE_ROWS, cols].astype(F32) for p in parts]
        for i in range(rows // BLOCK):
            each = []
            for lse in lses:
                total = lse[4 * i : 4 * i + 1] + lse[4 * i + 1 : 4 * i + 2] + lse[4 * i + 2 : 4 * i + 3]
                each.append(total)
            top = functools.reduce(jnp.maximum, each)
            shares = [jnp.exp2(e - top) for e in each]
            scale = 1.0 / functools.reduce(jnp.add, shares)
            here = slice(i * BLOCK, (i + 1) * BLOCK)
            mixed = jnp.zeros((BLOCK, HD), F32)
            for share, p in zip(shares, parts):
                column = jnp.transpose(jnp.broadcast_to(share * scale, (BLOCK, BLOCK)))
                mixed = mixed + column * p[here, cols].astype(F32)
            attn_ref[here, cols] = mixed.astype(BF16)

    for n in range(2 * NZ):
        out_ref = send_ref if n < NZ else keep_ref
        cols = columns(place, n, width)
        acc = jnp.dot(attn_ref[...], w_ref[:, cols], preferred_element_type=F32) + mlp_ref[n]
        out_ref[n % NZ] = acc.astype(BF16)


def branch(place, parts, mlp_branch, w_attn):
    _, rows, width = mlp_branch.shape
    return call(
        branch_kernel, [*parts, mlp_branch, w_attn], [((NZ, rows, width), BF16)] * 2,
        scalars=place, scratch=[VMEM((rows, width), BF16)], name="branch",
    )


def partner(kind, at, core):
    if kind == "opposite":
        return (at + 2) % 4
    step = 1 if at % 2 == 0 else 3
    if (kind == "second") != (core == 1):
        step = 4 - step
    return (at + step) % 4


def along(axis, kind, a):
    pairs = []
    for y in range(4):
        for x in range(4):
            for h in range(8):
                core = h % 2
                if (axis == "a") == (core == 0):
                    to = partner(kind, y, core) * 4 + x
                else:
                    to = y * 4 + partner(kind, x, core)
                pairs.append(((y * 4 + x) * 8 + h, to * 8 + h))
    return lax.ppermute(a, ("patch", "head"), pairs)


def up_or_down(a):
    return lax.ppermute(
        a, "head", [(z * 2 + c, (z + (1, 3)[c]) % 4 * 2 + c) for z in range(4) for c in range(2)]
    )


def along_z(a, k):
    return lax.ppermute(a, "head", [(z * 2 + c, (z + k) % 4 * 2 + c) for z in range(4) for c in range(2)])


def other_core(a):
    return lax.ppermute(a, "head", [(i, i ^ 1) for i in range(8)])


def ring(axis, a):
    first, second = along(axis, "first", a), along(axis, "second", a)
    return [a, first, second, along(axis, "second", first)]


def body(
    hidden, key_cache, value_cache, block_order, refresh_counts, modulation,
    query_gain, key_gain, w_qkv, w_mlp, w_out_attn, w_out_mlp,
):
    width = hidden.shape[1]
    count = refresh_counts[0]
    head = lax.axis_index("head")
    z, core = head // 2, head % 2
    place = jnp.stack([z, core, count]).astype(jnp.int32)
    w_qkv = jnp.transpose(w_qkv, (1, 0, 2))

    (rows,) = pick_rows(block_order, hidden)
    rest, old = pick_cache(block_order, key_cache, value_cache)
    rows, rest = lax.optimization_barrier((rows, rest))
    beside = other_core(rows)
    near = up_or_down(rows)
    near_beside = up_or_down(beside)
    across = up_or_down(near)
    pieces = [
        rows, beside, near, near_beside, across,
        other_core(near), other_core(near_beside), other_core(across),
    ]
    rest_first, rest_second = along("a", "first", rest), along("a", "second", rest)
    pieces, rest_first, rest_second = lax.optimization_barrier((pieces, rest_first, rest_second))
    rest = [rest, rest_first, rest_second, along("a", "second", rest_first)]

    query, fresh, modded = project(place, pieces, modulation, query_gain, key_gain, w_qkv, old)
    fresh, queries = ring("a", fresh), ring("b", query)
    mlp_hidden = mlp_in(modded, w_mlp)
    queries, mlp_hidden, fresh[1] = lax.optimization_barrier((queries, mlp_hidden, fresh[1]))
    state = attend(queries, rest, [], False)
    parts = attend(queries, fresh, state, True)
    mlp_branch = mlp_out(place, mlp_hidden, w_out_mlp)

    kinds = ("first", "second", "opposite")
    back = [parts[0]] + [along("b", kind, parts[n + 1]) for n, kind in enumerate(kinds)]
    send, keep = branch(place, back, mlp_branch, w_out_attn)
    chip = keep.astype(F32) + other_core(send).astype(F32)
    summed = chip[0]
    for k in (2, 1, 3):
        summed = summed + along_z(chip[k].astype(BF16), k).astype(F32)

    gate = lax.dynamic_slice_in_dim(modulation[2], head * width, width)
    result = (rows.astype(F32) + gate * summed).astype(BF16)
    live = jnp.arange(result.shape[0]) < count * BLOCK
    return jnp.where(live[:, None], result, jnp.zeros((), BF16))


def solution(mesh):
    in_specs = (
        P("patch", "head"), P("patch", "head"), P("patch", "head"), P("patch", None), P("patch"),
        P(), P(), P(),
        P(None, None, "head"), P(None, "head"), P("head", None), P("head", None),
    )
    return jax.shard_map(
        body, mesh=mesh, in_specs=in_specs, out_specs=P("patch", "head"), check_vma=False
    )
```

```python
import functools
import math

import jax
import jax.numpy as jnp
from jax import lax
from jax.experimental import pallas as pl
from jax.experimental.pallas import tpu as pltpu
from jax.sharding import PartitionSpec as P

HD = 128
BLOCK = 128
RMAX = 4
NZ = 4
SIDE = 4
LSE_ROWS = 16
NOTE_ROWS = 16
PER_US = 1_100_000_000
BF16 = jnp.bfloat16
F32 = jnp.float32
EXP2_SCALE = HD ** (-0.5) * math.log2(math.e)
VMEM = pltpu.VMEM


def spec(space):
    return pl.BlockSpec(memory_space=space)


def in_vmem(a):
    return pltpu.with_memory_space_constraint(a, VMEM)


def in_hbm(a):
    return pltpu.with_memory_space_constraint(a, pltpu.HBM)


def call(kernel, operands, outs, scalars=None, far=(), scratch=(), mib=16, cost=0, name=None):
    specs = [spec(VMEM)] * len(operands) + [spec(pltpu.HBM)] * len(far)
    operands = [in_vmem(a) for a in operands] + [in_hbm(a) for a in far]
    if scalars is not None:
        specs = [spec(pltpu.SMEM)] + specs
        operands = [scalars] + operands
    return pl.pallas_call(
        kernel,
        in_specs=specs,
        out_specs=[spec(VMEM)] * len(outs),
        out_shape=[VMEM(shape, dtype) for shape, dtype in outs],
        scratch_shapes=list(scratch),
        compiler_params=pltpu.CompilerParams(vmem_limit_bytes=mib * 2**20),
        cost_estimate=pl.CostEstimate(flops=cost, bytes_accessed=1000, transcendentals=0),
        name=name,
    )(*operands)


def copies_of(pairs, sems):
    copies = [pltpu.make_async_copy(src, dst, sems.at[n]) for n, (src, dst) in enumerate(pairs)]
    for copy in copies:
        copy.start()
    return copies


def block_at(order, place):
    return pl.ds(pl.multiple_of(order[0, place] * BLOCK, BLOCK), BLOCK)


def pick_kernel(order, hidden, keys, values, rows_ref, rest_ref, old_ref, sems):
    pairs = []
    width = keys.shape[1]
    for i in range(RMAX):
        pairs.append((hidden.at[block_at(order, i), :], rows_ref.at[pl.ds(i * BLOCK, BLOCK), :]))
    for i in range(2 * RMAX):
        here, to = block_at(order, (RMAX + i) % (2 * RMAX)), pl.ds(i % RMAX * BLOCK, BLOCK)
        for n, ref in enumerate((keys, values)):
            out = rest_ref if i < RMAX else old_ref
            pairs.append((ref.at[here, :], out.at[to, pl.ds(n * width, width)]))
    for copy in copies_of(pairs, sems):
        copy.wait()


def pick(order, hidden, keys, values):
    tall, width = RMAX * BLOCK, hidden.shape[1]
    return call(
        pick_kernel, [], [((tall, width), BF16)] + [((tall, 2 * width), BF16)] * 2, scalars=order,
        far=[hidden, keys, values], scratch=[pltpu.SemaphoreType.DMA((5 * RMAX,))], name="pick",
    )


def project_kernel(
    place, p0, p1, p2, p3, p4, p5, p6, p7, old_ref, mod_far, qg_far, kg_far, w_ref,
    q_ref, kv_ref, modded_ref, mod_ref, qg_ref, kg_ref, w_vmem, sems,
):
    pieces = (p0, p1, p2, p3, p4, p5, p6, p7)
    z, core, count = place[0], place[1], place[2]
    rows, width = p0.shape
    features = width * len(pieces)
    mod_copy, *weight_copies, qg_copy, kg_copy = copies_of(
        [(mod_far, mod_ref)] + [(w_ref.at[n], w_vmem.at[n]) for n in range(3)]
        + [(qg_far, qg_ref), (kg_far, kg_ref)],
        sems,
    )
    near = lax.rem(z + NZ - 1 + 2 * core, NZ)
    away = lax.rem(z + NZ + 1 - 2 * core, NZ)
    across = lax.rem(z + 2, NZ)
    homes = [zone * 2 + core for zone in (z, near, away, across)]
    homes += [zone * 2 + 1 - core for zone in (z, away, near, across)]
    mod_copy.wait()
    tall = 32

    def norm(i, carry):
        here = pl.ds(pl.multiple_of(i * tall, tall), tall)
        total = jnp.zeros((tall, width), F32)
        for n in range(8):
            total = total + pieces[n][here, :].astype(F32)
        mean = jnp.sum(total, axis=-1, keepdims=True) * (1.0 / features)
        square = jnp.zeros((tall, width), F32)
        for n in range(8):
            center = pieces[n][here, :].astype(F32) - mean
            square = square + center * center
        spread = jnp.sum(square, axis=-1, keepdims=True) * (1.0 / features)
        inv = lax.rsqrt(spread + 1e-06)
        for n, h in enumerate(homes):
            cols = pl.ds(pl.multiple_of(h * width, 128), width)
            normed = (pieces[n][here, :].astype(F32) - mean) * inv
            out = normed * (1.0 + mod_ref[1:2, cols]) + mod_ref[0:1, cols]
            modded_ref[here, cols] = out.astype(BF16)
        return carry

    lax.fori_loop(0, rows // tall, norm, 0, unroll=2)

    def rms(v, gain):
        scale = lax.rsqrt(jnp.mean(v * v, axis=-1, keepdims=True) + 1e-06)
        return v * scale * gain

    heads = width // HD
    waits = {0: [weight_copies[0], qg_copy, kg_copy], 2: [weight_copies[1]], 6: [weight_copies[2]]}
    for first in range(0, 3 * heads, 2):
        pair = range(first, min(first + 2, 3 * heads))
        for copy in waits.get(first, ()):
            copy.wait()
        for i in range(rows // 256):
            here = slice(i * 256, (i + 1) * 256)
            weights = [w_vmem[h // heads][:, h % heads * HD : (h % heads + 1) * HD] for h in pair]
            acc = jnp.dot(
                modded_ref[here, :], jnp.concatenate(weights, axis=1), preferred_element_type=F32
            )
            live = i * 256 + lax.broadcasted_iota(jnp.int32, (256, HD), 0) < count * BLOCK
            for n, h in enumerate(pair):
                v = acc[:, n * HD : (n + 1) * HD]
                if h < heads:
                    q_ref[here, h * HD : (h + 1) * HD] = rms(v, qg_ref[...]).astype(BF16)
                else:
                    cols = slice((h - heads) * HD, (h - heads + 1) * HD)
                    v = rms(v, kg_ref[...]) if h < 2 * heads else v
                    kv_ref[here, cols] = jnp.where(live, v, old_ref[here, cols].astype(F32)).astype(BF16)
    q_ref[rows : rows + NOTE_ROWS, :] = (
        jnp.full((NOTE_ROWS, width), count, jnp.int32).astype(F32).astype(BF16)
    )


def project(place, pieces, modulation, query_gain, key_gain, w_qkv, old):
    rows, width = pieces[0].shape
    features = w_qkv.shape[1]
    return call(
        project_kernel,
        [*pieces, old],
        [((rows + NOTE_ROWS, width), BF16), ((rows, 2 * width), BF16), ((rows, features), BF16)],
        scalars=place, far=[modulation, query_gain.reshape(1, HD), key_gain.reshape(1, HD), w_qkv],
        scratch=[
            VMEM(modulation.shape, F32), VMEM((1, HD), F32), VMEM((1, HD), F32), VMEM(w_qkv.shape, BF16),
            pltpu.SemaphoreType.DMA((6,)),
        ],
        cost=10 * PER_US, name="project",
    )


def mlp_kernel(modded_ref, w_ref, out_ref, w_vmem, sems):
    width = w_ref.shape[1] // 3
    tiles = [slice(j * width, (j + 1) * width) for j in range(3)]
    copies = copies_of(
        [(w_ref.at[:, pl.ds(j * width, width)], w_vmem.at[j]) for j in range(3)], sems
    )
    for j in range(3):
        copies[j].wait()
        for i in range(modded_ref.shape[0] // 256):
            here = slice(i * 256, (i + 1) * 256)
            acc = jnp.dot(modded_ref[here, :], w_vmem[j], preferred_element_type=F32)
            out_ref[here, tiles[j]] = jax.nn.gelu(acc, approximate=True).astype(BF16)


def mlp_in(modded, w_mlp):
    rows, features = modded.shape
    hidden = w_mlp.shape[1]
    return call(
        mlp_kernel, [modded], [((rows, hidden), BF16)], far=[w_mlp],
        scratch=[VMEM((3, features, hidden // 3), BF16), pltpu.SemaphoreType.DMA((3,))],
        cost=5 * PER_US, name="mlp_in",
    )[0]


def attend_kernel(*refs, n_keys, chained):
    refs = list(refs)

    def take(n):
        out = refs[:n]
        del refs[:n]
        return out

    q_refs, kv_refs = take(SIDE), take(n_keys)
    o_in, lse_in = take(2) if chained else (None, None)
    out_refs = take(SIDE) if chained else None
    o_out, lse_out, qs = take(3)
    rows, width = q_refs[0].shape[0] - NOTE_ROWS, q_refs[0].shape[1]
    slots, heads = rows // BLOCK, width // HD

    starts, live, total = [], [], 0
    for s in range(SIDE):
        count = jnp.max(q_refs[s][rows : rows + NOTE_ROWS, :HD].astype(F32)).astype(jnp.int32)
        starts.append(total)
        live.append(count)
        total = total + count

    for s in range(SIDE):
        for i in range(slots):
            @pl.when(i < live[s])
            def _(s=s, i=i):
                to = pl.ds(pl.multiple_of((starts[s] + i) * BLOCK, BLOCK), BLOCK)
                qs[to, :] = q_refs[s][i * BLOCK : (i + 1) * BLOCK, :]

    def lanes(j):
        return slice(j * HD, (j + 1) * HD)

    def tile(at, tall):
        here = pl.ds(pl.multiple_of(at * BLOCK, BLOCK), tall)

        def score(j):
            q = qs[here, lanes(j)]
            return [
                lax.dot_general(q, kv[:, lanes(j)], (((1,), (1,)), ((), ())), preferred_element_type=F32)
                for kv in kv_refs
            ]

        ahead = score(0)
        for j in range(heads):
            scores = ahead
            if j + 1 < heads:
                ahead = score(j + 1)
            top = functools.reduce(jnp.maximum, [jnp.max(s, axis=-1, keepdims=True) for s in scores])
            top = top * EXP2_SCALE
            if chained:
                lse = lse_in[here, lanes(j)]
                top = jnp.maximum(top, lse[:, :1])
                share = jnp.exp2(lse - top)
                acc = jnp.concatenate([o_in[here, lanes(j)] * share, share], axis=1)
            else:
                acc = jnp.zeros((tall, 2 * HD), F32)
            for s, kv in zip(scores, kv_refs):
                weights = jnp.exp2(s * EXP2_SCALE - top).astype(BF16)
                value = kv[:, width + j * HD : width + (j + 1) * HD]
                value = jnp.concatenate([value, jnp.ones(value.shape, BF16)], axis=1)
                acc = acc + jnp.dot(weights, value, preferred_element_type=F32)
            o_out[here, lanes(j)] = acc[:, :HD] / acc[:, HD:]
            lse_out[here, lanes(j)] = top + jnp.log2(acc[:, HD:])

    big = lax.div(total, 4)
    done = 4 * big

    def tall_tile(t, carry):
        tile(4 * t, 4 * BLOCK)
        return carry

    def short_tile(t, carry):
        tile(done + 2 * t, 2 * BLOCK)
        return carry

    lax.fori_loop(0, big, tall_tile, 0)
    lax.fori_loop(0, lax.div(total - done + 1, 2), short_tile, 0)
    if not chained:
        return

    line = lax.broadcasted_iota(jnp.int32, (LSE_ROWS, BLOCK), 0)
    for s in range(SIDE):
        out_refs[s][rows : rows + LSE_ROWS, :] = jnp.zeros((LSE_ROWS, width), BF16)
        for i in range(slots):
            @pl.when(i < live[s])
            def _(s=s, i=i):
                here = pl.ds(pl.multiple_of((starts[s] + i) * BLOCK, BLOCK), BLOCK)
                out_refs[s][i * BLOCK : (i + 1) * BLOCK, :] = o_out[here, :].astype(BF16)
                for j in range(heads):
                    lse = jnp.transpose(lse_out[here, lanes(j)])[:LSE_ROWS, :]
                    high = lse.astype(BF16).astype(F32)
                    mid = (lse - high).astype(BF16).astype(F32)
                    low = lse - high - mid
                    packed = out_refs[s][rows : rows + LSE_ROWS, lanes(j)].astype(F32)
                    part = line - 4 * i
                    packed = jnp.where(part == 0, high, packed)
                    packed = jnp.where(part == 1, mid, packed)
                    packed = jnp.where(part == 2, low, packed)
                    out_refs[s][rows : rows + LSE_ROWS, lanes(j)] = packed.astype(BF16)


def attend(queries, caches, state=()):
    tall, width = queries[0].shape
    rows = tall - NOTE_ROWS
    most = SIDE * rows + BLOCK
    states = [((most, width), F32)] * 2
    scratch = [VMEM((most, width), BF16)]
    if state:
        outs = [((rows + LSE_ROWS, width), BF16)] * SIDE
        scratch = [VMEM(shape, dtype) for shape, dtype in states] + scratch
    else:
        outs = states
    return call(
        functools.partial(attend_kernel, n_keys=len(caches), chained=bool(state)),
        [*queries, *caches, *state], outs, scratch=scratch, mib=24, cost=9 * PER_US if state else 0,
        name="attend_last" if state else "attend_first",
    )


CHUNKS = ("across", "near", "away", "own")


def columns(place, n, width):
    z, core = place[0], place[1]
    step = lax.rem(1 + 2 * core, NZ)
    if n >= NZ:
        step = NZ - step
    zone = lax.rem(z + (2, step, NZ - step, 0)[n % NZ], NZ)
    side = core if n < NZ else 1 - core
    return pl.ds(pl.multiple_of((zone * 2 + side) * width, 128), width)


def mlp_out_kernel(place, mlp_ref, w_ref, out_ref):
    for n in range(2 * NZ):
        cols = columns(place, n, out_ref.shape[2])
        out_ref[n] = jnp.dot(mlp_ref[...], w_ref[:, cols], preferred_element_type=F32)


def mlp_out(place, mlp_hidden, w_out):
    rows, hidden = mlp_hidden.shape
    width = w_out.shape[1] // (2 * NZ)
    return call(
        mlp_out_kernel, [mlp_hidden, w_out], [((2 * NZ, rows, width), F32)], scalars=place,
        cost=4 * PER_US, name="mlp_out",
    )[0]


def mix_kernel(p0, p1, p2, p3, attn_ref):
    parts = (p0, p1, p2, p3)
    rows, width = attn_ref.shape
    for j in range(width // HD):
        cols = slice(j * HD, (j + 1) * HD)
        lses = [p[rows : rows + LSE_ROWS, cols].astype(F32) for p in parts]
        for i in range(rows // BLOCK):
            each = []
            for lse in lses:
                total = lse[4 * i : 4 * i + 1] + lse[4 * i + 1 : 4 * i + 2] + lse[4 * i + 2 : 4 * i + 3]
                each.append(total)
            top = functools.reduce(jnp.maximum, each)
            shares = [jnp.exp2(e - top) for e in each]
            scale = 1.0 / functools.reduce(jnp.add, shares)
            here = slice(i * BLOCK, (i + 1) * BLOCK)
            mixed = jnp.zeros((BLOCK, HD), F32)
            for share, p in zip(shares, parts):
                column = jnp.transpose(jnp.broadcast_to(share * scale, (BLOCK, BLOCK)))
                mixed = mixed + column * p[here, cols].astype(F32)
            attn_ref[here, cols] = mixed.astype(BF16)


def chunk_dots(place, k, attn_ref, mlp_ref, w_ref, send_ref, keep_ref):
    width = attn_ref.shape[1]
    for n, out_ref in ((NZ + k, send_ref), (k, keep_ref)):
        cols = columns(place, n, width)
        acc = jnp.dot(attn_ref[...], w_ref[:, cols], preferred_element_type=F32) + mlp_ref[n]
        out_ref[...] = acc.astype(BF16)


def branch_first_kernel(place, p0, p1, p2, p3, mlp_ref, w_ref, attn_ref, send_ref, keep_ref, *, k):
    mix_kernel(p0, p1, p2, p3, attn_ref)
    chunk_dots(place, k, attn_ref, mlp_ref, w_ref, send_ref, keep_ref)


def branch_next_kernel(place, attn_ref, mlp_ref, w_ref, send_ref, keep_ref, *, k):
    chunk_dots(place, k, attn_ref, mlp_ref, w_ref, send_ref, keep_ref)


def branch(place, inputs, mlp_branch, w_attn, k):
    _, rows, width = mlp_branch.shape
    first = len(inputs) == SIDE
    return call(
        functools.partial(branch_first_kernel if first else branch_next_kernel, k=k),
        [*inputs, mlp_branch, w_attn], [((rows, width), BF16)] * (3 if first else 2),
        scalars=place, name="branch",
    )


def finish_kernel(place, rows_ref, mine_ref, s1, s2, gate_ref, out_ref):
    count = place[2]
    for i in range(rows_ref.shape[0] // BLOCK):
        here = slice(i * BLOCK, (i + 1) * BLOCK)
        total = mine_ref[here, :] + s1[here, :].astype(F32) + s2[here, :].astype(F32)
        result = rows_ref[here, :].astype(F32) + gate_ref[...] * total
        out_ref[here, :] = jnp.where(i < count, result, 0.0).astype(BF16)


def finish(place, rows, mine, sums, gate):
    operands = [in_vmem(a) for a in (rows, mine, *sums, gate)]
    return pl.pallas_call(
        finish_kernel,
        in_specs=[spec(pltpu.SMEM)] + [spec(VMEM)] * len(operands),
        out_specs=spec(VMEM),
        out_shape=jax.ShapeDtypeStruct(rows.shape, BF16),
        compiler_params=pltpu.CompilerParams(vmem_limit_bytes=16 * 2**20),
        name="finish",
    )(place, *operands)


def partner(kind, at, core):
    if kind == "opposite":
        return (at + 2) % 4
    step = 1 if at % 2 == 0 else 3
    if (kind == "second") != (core == 1):
        step = 4 - step
    return (at + step) % 4


def along(axis, kind, a):
    pairs = []
    for y in range(4):
        for x in range(4):
            for h in range(8):
                core = h % 2
                if (axis == "a") == (core == 0):
                    to = partner(kind, y, core) * 4 + x
                else:
                    to = y * 4 + partner(kind, x, core)
                pairs.append(((y * 4 + x) * 8 + h, to * 8 + h))
    return lax.ppermute(a, ("patch", "head"), pairs)


def up_or_down(a, steps=(1, 3)):
    return lax.ppermute(
        a, "head", [(z * 2 + c, (z + steps[c]) % 4 * 2 + c) for z in range(4) for c in range(2)]
    )


def along_z(a, k):
    return lax.ppermute(a, "head", [(z * 2 + c, (z + k) % 4 * 2 + c) for z in range(4) for c in range(2)])


def other_core(a):
    return lax.ppermute(a, "head", [(i, i ^ 1) for i in range(8)])


def ring_near(axis, a):
    return [a, along(axis, "first", a), along(axis, "second", a)]


def ring_far(axis, buffers):
    return [*buffers, along(axis, "second", buffers[1])]


def body(
    hidden, key_cache, value_cache, block_order, refresh_counts, modulation,
    query_gain, key_gain, w_qkv, w_mlp, w_out_attn, w_out_mlp,
):
    count = refresh_counts[0]
    head = lax.axis_index("head")
    z, core = head // 2, head % 2
    place = jnp.stack([z, core, count]).astype(jnp.int32)
    width = hidden.shape[1]
    gate = lax.dynamic_slice(modulation, (2, head * width), (1, width))
    w_qkv = jnp.transpose(w_qkv, (1, 0, 2))

    rows, rest, old = pick(block_order, hidden, key_cache, value_cache)
    near, away = up_or_down(rows), up_or_down(rows, (3, 1))
    own = [rows, near, away, up_or_down(near)]
    pieces = own + [other_core(a) for a in own]
    rest_first, rest_second = along("a", "first", rest), along("a", "second", rest)
    pieces, rest_first, rest_second = lax.optimization_barrier((pieces, rest_first, rest_second))
    rest_opposite = along("a", "second", rest_first)

    query, fresh, modded = project(place, pieces, modulation, query_gain, key_gain, w_qkv, old)
    query, fresh, modded, rest_opposite = lax.optimization_barrier((query, fresh, modded, rest_opposite))
    rest = [rest, rest_first, rest_second, rest_opposite]
    queries, fresh = ring_near("b", query), ring_near("a", fresh)
    mlp_hidden = mlp_in(modded, w_mlp)
    queries, mlp_hidden = lax.optimization_barrier((queries, mlp_hidden))
    queries = ring_far("b", queries)
    queries, fresh = lax.optimization_barrier((queries, fresh))
    fresh = ring_far("a", fresh)
    state = attend(queries, rest)
    parts = attend(queries, fresh, state)
    kinds = ("first", "second", "opposite")
    back = [parts[0]] + [along("b", kind, parts[n + 1]) for n, kind in enumerate(kinds)]
    mlp_branch = mlp_out(place, mlp_hidden, w_out_mlp)
    attn, send, keep = branch(place, back, mlp_branch, w_out_attn, 0)
    across = (keep.astype(F32) + other_core(send).astype(F32)).astype(BF16)
    attn, across = lax.optimization_barrier((attn, across))
    across = up_or_down(across)
    chips = []
    for k in (2, 1, 3):
        if k == 3:
            attn, across = lax.optimization_barrier((attn, across))
        send, keep = branch(place, [attn], mlp_branch, w_out_attn, k)
        chips.append(keep.astype(F32) + other_core(send).astype(F32))
    near = up_or_down((chips[1] + across.astype(F32)).astype(BF16))
    away = up_or_down(chips[0].astype(BF16), (3, 1))
    return finish(place, rows, chips[2], [near, away], gate)


def solution(mesh):
    in_specs = (
        P("patch", "head"), P("patch", "head"), P("patch", "head"), P("patch", None), P("patch"),
        P(), P(), P(),
        P(None, None, "head"), P(None, "head"), P("head", None), P("head", None),
    )
    return jax.shard_map(
        body, mesh=mesh, in_specs=in_specs, out_specs=P("patch", "head"), check_vma=False
    )
```

```python
import functools
import math

import jax
import jax.numpy as jnp
from jax import lax
from jax.experimental import pallas as pl
from jax.experimental.pallas import tpu as pltpu
from jax.sharding import PartitionSpec as P

HD = 128
BLOCK = 128
RMAX = 4
NZ = 4
SIDE = 4
LSE_ROWS = 16
NOTE_ROWS = 16
PER_US = 1_100_000_000
BF16 = jnp.bfloat16
F32 = jnp.float32
EXP2_SCALE = HD ** (-0.5) * math.log2(math.e)
VMEM = pltpu.VMEM


def spec(space):
    return pl.BlockSpec(memory_space=space)


def in_vmem(a):
    return pltpu.with_memory_space_constraint(a, VMEM)


def in_hbm(a):
    return pltpu.with_memory_space_constraint(a, pltpu.HBM)


def call(kernel, operands, outs, scalars=None, far=(), scratch=(), mib=16, cost=0, name=None):
    specs = [spec(VMEM)] * len(operands) + [spec(pltpu.HBM)] * len(far)
    operands = [in_vmem(a) for a in operands] + [in_hbm(a) for a in far]
    if scalars is not None:
        specs = [spec(pltpu.SMEM)] + specs
        operands = [scalars] + operands
    return pl.pallas_call(
        kernel,
        in_specs=specs,
        out_specs=[spec(VMEM)] * len(outs),
        out_shape=[VMEM(shape, dtype) for shape, dtype in outs],
        scratch_shapes=list(scratch),
        compiler_params=pltpu.CompilerParams(vmem_limit_bytes=mib * 2**20),
        cost_estimate=pl.CostEstimate(flops=cost, bytes_accessed=1000, transcendentals=0),
        name=name,
    )(*operands)


def copies_of(pairs, sems):
    copies = [pltpu.make_async_copy(src, dst, sems.at[n]) for n, (src, dst) in enumerate(pairs)]
    for copy in copies:
        copy.start()
    return copies


def block_at(order, place):
    return pl.ds(pl.multiple_of(order[0, place] * BLOCK, BLOCK), BLOCK)


def pick_kernel(order, hidden, keys, values, rows_ref, rest_ref, sems):
    pairs = []
    width = keys.shape[1]
    for i in range(RMAX):
        pairs.append((hidden.at[block_at(order, i), :], rows_ref.at[pl.ds(i * BLOCK, BLOCK), :]))
    for i in range(RMAX):
        here, to = block_at(order, RMAX + i), pl.ds(i * BLOCK, BLOCK)
        for n, ref in enumerate((keys, values)):
            pairs.append((ref.at[here, :], rest_ref.at[to, pl.ds(n * width, width)]))
    for copy in copies_of(pairs, sems):
        copy.wait()


def pick(order, hidden, keys, values):
    tall, width = RMAX * BLOCK, hidden.shape[1]
    return call(
        pick_kernel, [], [((tall, width), BF16), ((tall, 2 * width), BF16)], scalars=order,
        far=[hidden, keys, values], scratch=[pltpu.SemaphoreType.DMA((3 * RMAX,))], name="pick",
    )


def project_kernel(
    place, p0, p1, p2, p3, p4, p5, p6, p7, mod_far, qg_far, kg_far, w_ref, keys, values,
    q_ref, kv_ref, modded_ref, pieces_ref, old_ref, mod_ref, qg_ref, kg_ref, w_vmem, sems,
):
    z, core, count = place[0, 0], place[0, 1], place[0, 2]
    rows, width = p0.shape
    far_pieces = (p1, p2, p3, p4, p5, p6, p7)
    pieces = [p0] + [pieces_ref.at[n] for n in range(len(far_pieces))]
    features = width * len(pieces)
    copies = copies_of(
        [(ref, pieces_ref.at[n]) for n, ref in enumerate(far_pieces)]
        + [(mod_far, mod_ref), (qg_far, qg_ref), (kg_far, kg_ref)]
        + [(w_ref.at[n], w_vmem.at[n]) for n in range(3)]
        + [
            (ref.at[block_at(place, 3 + i), :], old_ref.at[pl.ds(i * BLOCK, BLOCK), pl.ds(n * width, width)])
            for i in range(RMAX)
            for n, ref in enumerate((keys, values))
        ],
        sems,
    )
    piece_copies, (mod_copy, qg_copy, kg_copy), weight_copies, old_copies = (
        copies[:7], copies[7:10], copies[10:13], copies[13:],
    )
    near = lax.rem(z + NZ - 1 + 2 * core, NZ)
    away = lax.rem(z + NZ + 1 - 2 * core, NZ)
    across = lax.rem(z + 2, NZ)
    homes = [zone * 2 + core for zone in (z, near, away, across)]
    homes += [zone * 2 + 1 - core for zone in (z, away, near, across)]
    for copy in (*piece_copies, mod_copy):
        copy.wait()
    tall = 32

    def norm(i, carry):
        here = pl.ds(pl.multiple_of(i * tall, tall), tall)
        total = jnp.zeros((tall, width), F32)
        for n in range(8):
            total = total + pieces[n][here, :].astype(F32)
        mean = jnp.sum(total, axis=-1, keepdims=True) * (1.0 / features)
        square = jnp.zeros((tall, width), F32)
        for n in range(8):
            center = pieces[n][here, :].astype(F32) - mean
            square = square + center * center
        spread = jnp.sum(square, axis=-1, keepdims=True) * (1.0 / features)
        inv = lax.rsqrt(spread + 1e-06)
        for n, h in enumerate(homes):
            cols = pl.ds(pl.multiple_of(h * width, 128), width)
            normed = (pieces[n][here, :].astype(F32) - mean) * inv
            out = normed * (1.0 + mod_ref[1:2, cols]) + mod_ref[0:1, cols]
            modded_ref[here, cols] = out.astype(BF16)
        return carry

    lax.fori_loop(0, rows // tall, norm, 0, unroll=2)

    def rms(v, gain):
        scale = lax.rsqrt(jnp.mean(v * v, axis=-1, keepdims=True) + 1e-06)
        return v * scale * gain

    heads = width // HD
    waits = {0: [weight_copies[0], qg_copy, kg_copy], 2: [weight_copies[1], *old_copies], 6: [weight_copies[2]]}
    for first in range(0, 3 * heads, 2):
        pair = range(first, min(first + 2, 3 * heads))
        for copy in waits.get(first, ()):
            copy.wait()
        for i in range(rows // 256):
            here = slice(i * 256, (i + 1) * 256)
            weights = [w_vmem[h // heads][:, h % heads * HD : (h % heads + 1) * HD] for h in pair]
            acc = jnp.dot(
                modded_ref[here, :], jnp.concatenate(weights, axis=1), preferred_element_type=F32
            )
            live = i * 256 + lax.broadcasted_iota(jnp.int32, (256, HD), 0) < count * BLOCK
            for n, h in enumerate(pair):
                v = acc[:, n * HD : (n + 1) * HD]
                if h < heads:
                    q_ref[here, h * HD : (h + 1) * HD] = rms(v, qg_ref[...]).astype(BF16)
                else:
                    cols = slice((h - heads) * HD, (h - heads + 1) * HD)
                    v = rms(v, kg_ref[...]) if h < 2 * heads else v
                    kv_ref[here, cols] = jnp.where(live, v, old_ref[here, cols].astype(F32)).astype(BF16)
    q_ref[rows : rows + NOTE_ROWS, :] = (
        jnp.full((NOTE_ROWS, width), count, jnp.int32).astype(F32).astype(BF16)
    )


def project(place, pieces, modulation, query_gain, key_gain, w_qkv, keys, values):
    rows, width = pieces[0].shape
    features = w_qkv.shape[1]
    return call(
        project_kernel,
        pieces[:1],
        [((rows + NOTE_ROWS, width), BF16), ((rows, 2 * width), BF16), ((rows, features), BF16)],
        scalars=place, far=[
            *pieces[1:], modulation, query_gain.reshape(1, HD), key_gain.reshape(1, HD), w_qkv, keys, values,
        ],
        scratch=[
            VMEM((7, rows, width), BF16), VMEM((rows, 2 * width), BF16),
            VMEM(modulation.shape, F32), VMEM((1, HD), F32), VMEM((1, HD), F32), VMEM(w_qkv.shape, BF16),
            pltpu.SemaphoreType.DMA((13 + 2 * RMAX,)),
        ],
        cost=10 * PER_US, mib=24, name="project",
    )


def mlp_kernel(modded_ref, w_ref, out_ref, w_vmem, sems):
    width = w_ref.shape[1] // 3
    tiles = [slice(j * width, (j + 1) * width) for j in range(3)]
    copies = copies_of(
        [(w_ref.at[:, pl.ds(j * width, width)], w_vmem.at[j]) for j in range(3)], sems
    )
    for j in range(3):
        copies[j].wait()
        for i in range(modded_ref.shape[0] // 256):
            here = slice(i * 256, (i + 1) * 256)
            acc = jnp.dot(modded_ref[here, :], w_vmem[j], preferred_element_type=F32)
            out_ref[here, tiles[j]] = jax.nn.gelu(acc, approximate=True).astype(BF16)


def mlp_in(modded, w_mlp):
    rows, features = modded.shape
    hidden = w_mlp.shape[1]
    return call(
        mlp_kernel, [modded], [((rows, hidden), BF16)], far=[w_mlp],
        scratch=[VMEM((3, features, hidden // 3), BF16), pltpu.SemaphoreType.DMA((3,))],
        cost=5 * PER_US, name="mlp_in",
    )[0]


def attend_kernel(*refs, n_keys, chained):
    refs = list(refs)

    def take(n):
        out = refs[:n]
        del refs[:n]
        return out

    q_refs, kv_refs = take(SIDE), take(n_keys)
    o_in, lse_in = take(2) if chained else (None, None)
    out_refs = take(SIDE) if chained else None
    o_out, lse_out, qs = take(3)
    rows, width = q_refs[0].shape[0] - NOTE_ROWS, q_refs[0].shape[1]
    slots, heads = rows // BLOCK, width // HD

    starts, live, total = [], [], 0
    for s in range(SIDE):
        count = jnp.max(q_refs[s][rows : rows + NOTE_ROWS, :HD].astype(F32)).astype(jnp.int32)
        starts.append(total)
        live.append(count)
        total = total + count

    for s in range(SIDE):
        for i in range(slots):
            @pl.when(i < live[s])
            def _(s=s, i=i):
                to = pl.ds(pl.multiple_of((starts[s] + i) * BLOCK, BLOCK), BLOCK)
                qs[to, :] = q_refs[s][i * BLOCK : (i + 1) * BLOCK, :]

    def lanes(j):
        return slice(j * HD, (j + 1) * HD)

    def tile(at, tall):
        here = pl.ds(pl.multiple_of(at * BLOCK, BLOCK), tall)

        def score(j):
            q = qs[here, lanes(j)]
            return [
                lax.dot_general(q, kv[:, lanes(j)], (((1,), (1,)), ((), ())), preferred_element_type=F32)
                for kv in kv_refs
            ]

        ahead = score(0)
        for j in range(heads):
            scores = ahead
            if j + 1 < heads:
                ahead = score(j + 1)
            top = functools.reduce(jnp.maximum, [jnp.max(s, axis=-1, keepdims=True) for s in scores])
            top = top * EXP2_SCALE
            if chained:
                lse = lse_in[here, lanes(j)]
                top = jnp.maximum(top, lse[:, :1])
                share = jnp.exp2(lse - top)
                acc = jnp.concatenate([o_in[here, lanes(j)] * share, share], axis=1)
            else:
                acc = jnp.zeros((tall, 2 * HD), F32)
            for s, kv in zip(scores, kv_refs):
                weights = jnp.exp2(s * EXP2_SCALE - top).astype(BF16)
                value = kv[:, width + j * HD : width + (j + 1) * HD]
                value = jnp.concatenate([value, jnp.ones(value.shape, BF16)], axis=1)
                acc = acc + jnp.dot(weights, value, preferred_element_type=F32)
            o_out[here, lanes(j)] = acc[:, :HD] / acc[:, HD:]
            lse_out[here, lanes(j)] = top + jnp.log2(acc[:, HD:])

    big = lax.div(total, 4)
    done = 4 * big

    def tall_tile(t, carry):
        tile(4 * t, 4 * BLOCK)
        return carry

    def short_tile(t, carry):
        tile(done + 2 * t, 2 * BLOCK)
        return carry

    lax.fori_loop(0, big, tall_tile, 0)
    lax.fori_loop(0, lax.div(total - done + 1, 2), short_tile, 0)
    if not chained:
        return

    line = lax.broadcasted_iota(jnp.int32, (LSE_ROWS, BLOCK), 0)
    for s in range(SIDE):
        out_refs[s][rows : rows + LSE_ROWS, :] = jnp.zeros((LSE_ROWS, width), BF16)
        for i in range(slots):
            @pl.when(i < live[s])
            def _(s=s, i=i):
                here = pl.ds(pl.multiple_of((starts[s] + i) * BLOCK, BLOCK), BLOCK)
                out_refs[s][i * BLOCK : (i + 1) * BLOCK, :] = o_out[here, :].astype(BF16)
                for j in range(heads):
                    lse = jnp.transpose(lse_out[here, lanes(j)])[:LSE_ROWS, :]
                    high = lse.astype(BF16).astype(F32)
                    mid = (lse - high).astype(BF16).astype(F32)
                    low = lse - high - mid
                    packed = out_refs[s][rows : rows + LSE_ROWS, lanes(j)].astype(F32)
                    part = line - 4 * i
                    packed = jnp.where(part == 0, high, packed)
                    packed = jnp.where(part == 1, mid, packed)
                    packed = jnp.where(part == 2, low, packed)
                    out_refs[s][rows : rows + LSE_ROWS, lanes(j)] = packed.astype(BF16)


def attend(queries, caches, state=()):
    tall, width = queries[0].shape
    rows = tall - NOTE_ROWS
    most = SIDE * rows + BLOCK
    states = [((most, width), F32)] * 2
    scratch = [VMEM((most, width), BF16)]
    if state:
        outs = [((rows + LSE_ROWS, width), BF16)] * SIDE
        scratch = [VMEM(shape, dtype) for shape, dtype in states] + scratch
    else:
        outs = states
    return call(
        functools.partial(attend_kernel, n_keys=len(caches), chained=bool(state)),
        [*queries, *caches, *state], outs, scratch=scratch, mib=24, cost=9 * PER_US if state else 5 * PER_US,
        name="attend_last" if state else "attend_first",
    )


CHUNKS = ("across", "near", "away", "own")


def columns(place, n, width):
    z, core = place[0], place[1]
    step = lax.rem(1 + 2 * core, NZ)
    if n >= NZ:
        step = NZ - step
    zone = lax.rem(z + (2, step, NZ - step, 0)[n % NZ], NZ)
    side = core if n < NZ else 1 - core
    return pl.ds(pl.multiple_of((zone * 2 + side) * width, 128), width)


def mlp_out_kernel(place, mlp_ref, w_ref, out_ref):
    for n in range(2 * NZ):
        cols = columns(place, n, out_ref.shape[2])
        out_ref[n] = jnp.dot(mlp_ref[...], w_ref[:, cols], preferred_element_type=F32)


def mlp_out(place, mlp_hidden, w_out):
    rows, hidden = mlp_hidden.shape
    width = w_out.shape[1] // (2 * NZ)
    return call(
        mlp_out_kernel, [mlp_hidden, w_out], [((2 * NZ, rows, width), F32)], scalars=place,
        cost=4 * PER_US, name="mlp_out",
    )[0]


def mix_kernel(p0, p1, p2, p3, attn_ref):
    parts = (p0, p1, p2, p3)
    rows, width = attn_ref.shape
    for j in range(width // HD):
        cols = slice(j * HD, (j + 1) * HD)
        lses = [p[rows : rows + LSE_ROWS, cols].astype(F32) for p in parts]
        for i in range(rows // BLOCK):
            each = []
            for lse in lses:
                total = lse[4 * i : 4 * i + 1] + lse[4 * i + 1 : 4 * i + 2] + lse[4 * i + 2 : 4 * i + 3]
                each.append(total)
            top = functools.reduce(jnp.maximum, each)
            shares = [jnp.exp2(e - top) for e in each]
            scale = 1.0 / functools.reduce(jnp.add, shares)
            here = slice(i * BLOCK, (i + 1) * BLOCK)
            mixed = jnp.zeros((BLOCK, HD), F32)
            for share, p in zip(shares, parts):
                column = jnp.transpose(jnp.broadcast_to(share * scale, (BLOCK, BLOCK)))
                mixed = mixed + column * p[here, cols].astype(F32)
            attn_ref[here, cols] = mixed.astype(BF16)


def chunk_dots(place, k, attn_ref, mlp_ref, w_ref, send_ref, keep_ref):
    width = attn_ref.shape[1]
    for n, out_ref in ((NZ + k, send_ref), (k, keep_ref)):
        cols = columns(place, n, width)
        acc = jnp.dot(attn_ref[...], w_ref[:, cols], preferred_element_type=F32) + mlp_ref[n]
        out_ref[...] = acc.astype(BF16)


def branch_first_kernel(place, p0, p1, p2, p3, mlp_ref, w_ref, attn_ref, send_ref, keep_ref, *, k):
    mix_kernel(p0, p1, p2, p3, attn_ref)
    chunk_dots(place, k, attn_ref, mlp_ref, w_ref, send_ref, keep_ref)


def branch_next_kernel(place, attn_ref, mlp_ref, w_ref, send_ref, keep_ref, *, k):
    chunk_dots(place, k, attn_ref, mlp_ref, w_ref, send_ref, keep_ref)


def branch(place, inputs, mlp_branch, w_attn, k):
    _, rows, width = mlp_branch.shape
    first = len(inputs) == SIDE
    return call(
        functools.partial(branch_first_kernel if first else branch_next_kernel, k=k),
        [*inputs, mlp_branch, w_attn], [((rows, width), BF16)] * (3 if first else 2),
        scalars=place, name="branch",
    )


def finish_kernel(place, rows_ref, mine_ref, s1, s2, gate_ref, out_ref):
    count = place[2]
    for i in range(rows_ref.shape[0] // BLOCK):
        here = slice(i * BLOCK, (i + 1) * BLOCK)
        total = mine_ref[here, :] + s1[here, :].astype(F32) + s2[here, :].astype(F32)
        result = rows_ref[here, :].astype(F32) + gate_ref[...] * total
        out_ref[here, :] = jnp.where(i < count, result, 0.0).astype(BF16)


def finish(place, rows, mine, sums, gate):
    operands = [in_vmem(a) for a in (rows, mine, *sums, gate)]
    return pl.pallas_call(
        finish_kernel,
        in_specs=[spec(pltpu.SMEM)] + [spec(VMEM)] * len(operands),
        out_specs=spec(VMEM),
        out_shape=jax.ShapeDtypeStruct(rows.shape, BF16),
        compiler_params=pltpu.CompilerParams(vmem_limit_bytes=16 * 2**20),
        name="finish",
    )(place, *operands)


def partner(kind, at, core):
    if kind == "opposite":
        return (at + 2) % 4
    step = 1 if at % 2 == 0 else 3
    if (kind == "second") != (core == 1):
        step = 4 - step
    return (at + step) % 4


def along(axis, kind, a):
    pairs = []
    for y in range(4):
        for x in range(4):
            for h in range(8):
                core = h % 2
                if (axis == "a") == (core == 0):
                    to = partner(kind, y, core) * 4 + x
                else:
                    to = y * 4 + partner(kind, x, core)
                pairs.append(((y * 4 + x) * 8 + h, to * 8 + h))
    return lax.ppermute(a, ("patch", "head"), pairs)


def up_or_down(a, steps=(1, 3)):
    return lax.ppermute(
        a, "head", [(z * 2 + c, (z + steps[c]) % 4 * 2 + c) for z in range(4) for c in range(2)]
    )


def along_z(a, k):
    return lax.ppermute(a, "head", [(z * 2 + c, (z + k) % 4 * 2 + c) for z in range(4) for c in range(2)])


def other_core(a):
    return lax.ppermute(a, "head", [(i, i ^ 1) for i in range(8)])


def ring_near(axis, a):
    return [a, along(axis, "first", a), along(axis, "second", a)]


def ring_far(axis, buffers):
    return [*buffers, along(axis, "second", buffers[1])]


def body(
    hidden, key_cache, value_cache, block_order, refresh_counts, modulation,
    query_gain, key_gain, w_qkv, w_mlp, w_out_attn, w_out_mlp,
):
    count = refresh_counts[0]
    head = lax.axis_index("head")
    z, core = head // 2, head % 2
    place = jnp.stack([z, core, count]).astype(jnp.int32)
    ordered = jnp.concatenate([place, block_order[0, :RMAX]]).reshape(1, 3 + RMAX)
    width = hidden.shape[1]
    gate = lax.dynamic_slice(modulation, (2, head * width), (1, width))
    w_qkv = jnp.transpose(w_qkv, (1, 0, 2))

    rows, rest = pick(block_order, hidden, key_cache, value_cache)
    near, away = up_or_down(rows), up_or_down(rows, (3, 1))
    own = [rows, near, away, up_or_down(near)]
    pieces = own + [other_core(a) for a in own]
    rest_first, rest_second = along("a", "first", rest), along("a", "second", rest)
    pieces, rest_first, rest_second = lax.optimization_barrier((pieces, rest_first, rest_second))
    rest_opposite = along("a", "second", rest_first)

    query, fresh, modded = project(
        ordered, pieces, modulation, query_gain, key_gain, w_qkv, key_cache, value_cache
    )
    query, fresh, modded, rest_opposite = lax.optimization_barrier((query, fresh, modded, rest_opposite))
    rest = [rest, rest_first, rest_second, rest_opposite]
    queries, fresh = ring_near("b", query), ring_near("a", fresh)
    mlp_hidden = mlp_in(modded, w_mlp)
    queries, mlp_hidden = lax.optimization_barrier((queries, mlp_hidden))
    fresh = lax.optimization_barrier(fresh)
    queries, fresh = ring_far("b", queries), ring_far("a", fresh)
    state = attend(queries, rest)
    parts = attend(queries, fresh, state)
    kinds = ("first", "second", "opposite")
    back = [parts[0]] + [along("b", kind, parts[n + 1]) for n, kind in enumerate(kinds)]
    mlp_branch = mlp_out(place, mlp_hidden, w_out_mlp)
    attn, send, keep = branch(place, back, mlp_branch, w_out_attn, 0)
    across = (keep.astype(F32) + other_core(send).astype(F32)).astype(BF16)
    attn, across = lax.optimization_barrier((attn, across))
    across = up_or_down(across)
    chips = []
    for k in (2, 1, 3):
        if k == 3:
            attn, across = lax.optimization_barrier((attn, across))
        send, keep = branch(place, [attn], mlp_branch, w_out_attn, k)
        chips.append(keep.astype(F32) + other_core(send).astype(F32))
    near = up_or_down((chips[1] + across.astype(F32)).astype(BF16))
    away = up_or_down(chips[0].astype(BF16), (3, 1))
    return finish(place, rows, chips[2], [near, away], gate)


def solution(mesh):
    in_specs = (
        P("patch", "head"), P("patch", "head"), P("patch", "head"), P("patch", None), P("patch"),
        P(), P(), P(),
        P(None, None, "head"), P(None, "head"), P("head", None), P("head", None),
    )
    return jax.shard_map(
        body, mesh=mesh, in_specs=in_specs, out_specs=P("patch", "head"), check_vma=False
    )
```

```python
import functools
import math

import jax
import jax.numpy as jnp
from jax import lax
from jax.experimental import pallas as pl
from jax.experimental.pallas import tpu as pltpu
from jax.sharding import PartitionSpec as P

HD = 128
BLOCK = 128
RMAX = 4
NZ = 4
SIDE = 4
LSE_ROWS = 16
NOTE_ROWS = 16
PER_US = 1_100_000_000
BF16 = jnp.bfloat16
F32 = jnp.float32
EXP2_SCALE = HD ** (-0.5) * math.log2(math.e)
VMEM = pltpu.VMEM


def spec(space):
    return pl.BlockSpec(memory_space=space)


def in_vmem(a):
    return pltpu.with_memory_space_constraint(a, VMEM)


def in_hbm(a):
    return pltpu.with_memory_space_constraint(a, pltpu.HBM)


def call(kernel, operands, outs, scalars=None, far=(), scratch=(), mib=16, cost=0, name=None):
    specs = [spec(VMEM)] * len(operands) + [spec(pltpu.HBM)] * len(far)
    operands = [in_vmem(a) for a in operands] + [in_hbm(a) for a in far]
    if scalars is not None:
        specs = [spec(pltpu.SMEM)] + specs
        operands = [scalars] + operands
    return pl.pallas_call(
        kernel,
        in_specs=specs,
        out_specs=[spec(VMEM)] * len(outs),
        out_shape=[VMEM(shape, dtype) for shape, dtype in outs],
        scratch_shapes=list(scratch),
        compiler_params=pltpu.CompilerParams(vmem_limit_bytes=mib * 2**20),
        cost_estimate=pl.CostEstimate(flops=cost, bytes_accessed=1000, transcendentals=0),
        name=name,
    )(*operands)


def copies_of(pairs, sems):
    copies = [pltpu.make_async_copy(src, dst, sems.at[n]) for n, (src, dst) in enumerate(pairs)]
    for copy in copies:
        copy.start()
    return copies


def block_at(order, place):
    return pl.ds(pl.multiple_of(order[0, place] * BLOCK, BLOCK), BLOCK)


def pick_kernel(order, hidden, keys, values, rows_ref, rest_ref, sems):
    pairs = []
    width = keys.shape[1]
    for i in range(RMAX):
        pairs.append((hidden.at[block_at(order, i), :], rows_ref.at[pl.ds(i * BLOCK, BLOCK), :]))
    for i in range(RMAX):
        here, to = block_at(order, RMAX + i), pl.ds(i * BLOCK, BLOCK)
        for n, ref in enumerate((keys, values)):
            pairs.append((ref.at[here, :], rest_ref.at[to, pl.ds(n * width, width)]))
    for copy in copies_of(pairs, sems):
        copy.wait()


def pick(order, hidden, keys, values):
    tall, width = RMAX * BLOCK, hidden.shape[1]
    return call(
        pick_kernel, [], [((tall, width), BF16), ((tall, 2 * width), BF16)], scalars=order,
        far=[hidden, keys, values], scratch=[pltpu.SemaphoreType.DMA((3 * RMAX,))], name="pick",
    )


def project_kernel(
    place, p0, p1, p2, p3, p4, p5, p6, p7, mod_far, qg_far, kg_far, w_ref, keys, values,
    q_ref, kv_ref, modded_ref, pieces_ref, old_ref, mod_ref, qg_ref, kg_ref, w_vmem, sems,
):
    z, core, count = place[0, 0], place[0, 1], place[0, 2]
    rows, width = p0.shape
    far_pieces = (p1, p2, p3, p4, p5, p6, p7)
    pieces = [p0] + [pieces_ref.at[n] for n in range(len(far_pieces))]
    features = width * len(pieces)
    copies = copies_of(
        [(ref, pieces_ref.at[n]) for n, ref in enumerate(far_pieces)]
        + [(mod_far, mod_ref), (qg_far, qg_ref), (kg_far, kg_ref)]
        + [(w_ref.at[n], w_vmem.at[n]) for n in range(3)]
        + [
            (ref.at[block_at(place, 3 + i), :], old_ref.at[pl.ds(i * BLOCK, BLOCK), pl.ds(n * width, width)])
            for i in range(RMAX)
            for n, ref in enumerate((keys, values))
        ],
        sems,
    )
    piece_copies, (mod_copy, qg_copy, kg_copy), weight_copies, old_copies = (
        copies[:7], copies[7:10], copies[10:13], copies[13:],
    )
    near = lax.rem(z + NZ - 1 + 2 * core, NZ)
    away = lax.rem(z + NZ + 1 - 2 * core, NZ)
    across = lax.rem(z + 2, NZ)
    homes = [zone * 2 + core for zone in (z, near, away, across)]
    homes += [zone * 2 + 1 - core for zone in (z, away, near, across)]
    for copy in (*piece_copies, mod_copy):
        copy.wait()
    tall = 32

    def norm(i, carry):
        here = pl.ds(pl.multiple_of(i * tall, tall), tall)
        total = jnp.zeros((tall, width), F32)
        for n in range(8):
            total = total + pieces[n][here, :].astype(F32)
        mean = jnp.sum(total, axis=-1, keepdims=True) * (1.0 / features)
        square = jnp.zeros((tall, width), F32)
        for n in range(8):
            center = pieces[n][here, :].astype(F32) - mean
            square = square + center * center
        spread = jnp.sum(square, axis=-1, keepdims=True) * (1.0 / features)
        inv = lax.rsqrt(spread + 1e-06)
        for n, h in enumerate(homes):
            cols = pl.ds(pl.multiple_of(h * width, 128), width)
            normed = (pieces[n][here, :].astype(F32) - mean) * inv
            out = normed * (1.0 + mod_ref[1:2, cols]) + mod_ref[0:1, cols]
            modded_ref[here, cols] = out.astype(BF16)
        return carry

    lax.fori_loop(0, rows // tall, norm, 0, unroll=2)

    def rms(v, gain):
        scale = lax.rsqrt(jnp.mean(v * v, axis=-1, keepdims=True) + 1e-06)
        return v * scale * gain

    heads = width // HD
    waits = {0: [weight_copies[0], qg_copy, kg_copy], 2: [weight_copies[1], *old_copies], 6: [weight_copies[2]]}
    for first in range(0, 3 * heads, 2):
        pair = range(first, min(first + 2, 3 * heads))
        for copy in waits.get(first, ()):
            copy.wait()
        for i in range(rows // 256):
            here = slice(i * 256, (i + 1) * 256)
            weights = [w_vmem[h // heads][:, h % heads * HD : (h % heads + 1) * HD] for h in pair]
            acc = jnp.dot(
                modded_ref[here, :], jnp.concatenate(weights, axis=1), preferred_element_type=F32
            )
            live = i * 256 + lax.broadcasted_iota(jnp.int32, (256, HD), 0) < count * BLOCK
            for n, h in enumerate(pair):
                v = acc[:, n * HD : (n + 1) * HD]
                if h < heads:
                    q_ref[here, h * HD : (h + 1) * HD] = rms(v, qg_ref[...]).astype(BF16)
                else:
                    cols = slice((h - heads) * HD, (h - heads + 1) * HD)
                    v = rms(v, kg_ref[...]) if h < 2 * heads else v
                    kv_ref[here, cols] = jnp.where(live, v, old_ref[here, cols].astype(F32)).astype(BF16)
    q_ref[rows : rows + NOTE_ROWS, :] = (
        jnp.full((NOTE_ROWS, width), count, jnp.int32).astype(F32).astype(BF16)
    )


def project(place, pieces, modulation, query_gain, key_gain, w_qkv, keys, values):
    rows, width = pieces[0].shape
    features = w_qkv.shape[1]
    return call(
        project_kernel,
        pieces[:1],
        [((rows + NOTE_ROWS, width), BF16), ((rows, 2 * width), BF16), ((rows, features), BF16)],
        scalars=place, far=[
            *pieces[1:], modulation, query_gain.reshape(1, HD), key_gain.reshape(1, HD), w_qkv, keys, values,
        ],
        scratch=[
            VMEM((7, rows, width), BF16), VMEM((rows, 2 * width), BF16),
            VMEM(modulation.shape, F32), VMEM((1, HD), F32), VMEM((1, HD), F32), VMEM(w_qkv.shape, BF16),
            pltpu.SemaphoreType.DMA((13 + 2 * RMAX,)),
        ],
        cost=10 * PER_US, mib=24, name="project",
    )


def mlp_kernel(modded_ref, w_ref, out_ref, w_vmem, sems):
    width = w_ref.shape[1] // 3
    tiles = [slice(j * width, (j + 1) * width) for j in range(3)]
    copies = copies_of(
        [(w_ref.at[:, pl.ds(j * width, width)], w_vmem.at[j]) for j in range(3)], sems
    )
    for j in range(3):
        copies[j].wait()
        for i in range(modded_ref.shape[0] // 256):
            here = slice(i * 256, (i + 1) * 256)
            acc = jnp.dot(modded_ref[here, :], w_vmem[j], preferred_element_type=F32)
            out_ref[here, tiles[j]] = jax.nn.gelu(acc, approximate=True).astype(BF16)


def mlp_in(modded, w_mlp):
    rows, features = modded.shape
    hidden = w_mlp.shape[1]
    return call(
        mlp_kernel, [modded], [((rows, hidden), BF16)], far=[w_mlp],
        scratch=[VMEM((3, features, hidden // 3), BF16), pltpu.SemaphoreType.DMA((3,))],
        cost=8 * PER_US, name="mlp_in",
    )[0]


def attend_kernel(*refs, n_keys, chained):
    refs = list(refs)

    def take(n):
        out = refs[:n]
        del refs[:n]
        return out

    q_refs, kv_refs = take(SIDE), take(n_keys)
    o_in, lse_in = take(2) if chained else (None, None)
    out_refs = take(SIDE) if chained else None
    o_out, lse_out, qs = take(3)
    rows, width = q_refs[0].shape[0] - NOTE_ROWS, q_refs[0].shape[1]
    slots, heads = rows // BLOCK, width // HD

    starts, live, total = [], [], 0
    for s in range(SIDE):
        count = jnp.max(q_refs[s][rows : rows + NOTE_ROWS, :HD].astype(F32)).astype(jnp.int32)
        starts.append(total)
        live.append(count)
        total = total + count

    for s in range(SIDE):
        for i in range(slots):
            @pl.when(i < live[s])
            def _(s=s, i=i):
                to = pl.ds(pl.multiple_of((starts[s] + i) * BLOCK, BLOCK), BLOCK)
                qs[to, :] = q_refs[s][i * BLOCK : (i + 1) * BLOCK, :]

    def lanes(j):
        return slice(j * HD, (j + 1) * HD)

    def tile(at, tall):
        here = pl.ds(pl.multiple_of(at * BLOCK, BLOCK), tall)

        def score(j):
            q = qs[here, lanes(j)]
            return [
                lax.dot_general(q, kv[:, lanes(j)], (((1,), (1,)), ((), ())), preferred_element_type=F32)
                for kv in kv_refs
            ]

        ahead = score(0)
        for j in range(heads):
            scores = ahead
            if j + 1 < heads:
                ahead = score(j + 1)
            top = functools.reduce(jnp.maximum, [jnp.max(s, axis=-1, keepdims=True) for s in scores])
            top = top * EXP2_SCALE
            if chained:
                lse = lse_in[here, lanes(j)]
                top = jnp.maximum(top, lse[:, :1])
                share = jnp.exp2(lse - top)
                acc = jnp.concatenate([o_in[here, lanes(j)] * share, share], axis=1)
            else:
                acc = jnp.zeros((tall, 2 * HD), F32)
            for s, kv in zip(scores, kv_refs):
                weights = jnp.exp2(s * EXP2_SCALE - top).astype(BF16)
                value = kv[:, width + j * HD : width + (j + 1) * HD]
                value = jnp.concatenate([value, jnp.ones(value.shape, BF16)], axis=1)
                acc = acc + jnp.dot(weights, value, preferred_element_type=F32)
            o_out[here, lanes(j)] = acc[:, :HD] / acc[:, HD:]
            lse_out[here, lanes(j)] = top + jnp.log2(acc[:, HD:])

    big = lax.div(total, 4)
    done = 4 * big

    def tall_tile(t, carry):
        tile(4 * t, 4 * BLOCK)
        return carry

    def short_tile(t, carry):
        tile(done + 2 * t, 2 * BLOCK)
        return carry

    lax.fori_loop(0, big, tall_tile, 0)
    lax.fori_loop(0, lax.div(total - done + 1, 2), short_tile, 0)
    if not chained:
        return

    line = lax.broadcasted_iota(jnp.int32, (LSE_ROWS, BLOCK), 0)
    for s in range(SIDE):
        out_refs[s][rows : rows + LSE_ROWS, :] = jnp.zeros((LSE_ROWS, width), BF16)
        for i in range(slots):
            @pl.when(i < live[s])
            def _(s=s, i=i):
                here = pl.ds(pl.multiple_of((starts[s] + i) * BLOCK, BLOCK), BLOCK)
                out_refs[s][i * BLOCK : (i + 1) * BLOCK, :] = o_out[here, :].astype(BF16)
                for j in range(heads):
                    lse = jnp.transpose(lse_out[here, lanes(j)])[:LSE_ROWS, :]
                    high = lse.astype(BF16).astype(F32)
                    mid = (lse - high).astype(BF16).astype(F32)
                    low = lse - high - mid
                    packed = out_refs[s][rows : rows + LSE_ROWS, lanes(j)].astype(F32)
                    part = line - 4 * i
                    packed = jnp.where(part == 0, high, packed)
                    packed = jnp.where(part == 1, mid, packed)
                    packed = jnp.where(part == 2, low, packed)
                    out_refs[s][rows : rows + LSE_ROWS, lanes(j)] = packed.astype(BF16)


def attend(queries, caches, state=()):
    tall, width = queries[0].shape
    rows = tall - NOTE_ROWS
    most = SIDE * rows + BLOCK
    states = [((most, width), F32)] * 2
    scratch = [VMEM((most, width), BF16)]
    if state:
        outs = [((rows + LSE_ROWS, width), BF16)] * SIDE
        scratch = [VMEM(shape, dtype) for shape, dtype in states] + scratch
    else:
        outs = states
    return call(
        functools.partial(attend_kernel, n_keys=len(caches), chained=bool(state)),
        [*queries, *caches, *state], outs, scratch=scratch, mib=24, cost=9 * PER_US if state else 5 * PER_US,
        name="attend_last" if state else "attend_first",
    )


CHUNKS = ("across", "near", "away", "own")


def columns(place, n, width):
    z, core = place[0], place[1]
    step = lax.rem(1 + 2 * core, NZ)
    if n >= NZ:
        step = NZ - step
    zone = lax.rem(z + (2, step, NZ - step, 0)[n % NZ], NZ)
    side = core if n < NZ else 1 - core
    return pl.ds(pl.multiple_of((zone * 2 + side) * width, 128), width)


def mlp_out_kernel(place, mlp_ref, w_ref, out_ref):
    for n in range(2 * NZ):
        cols = columns(place, n, out_ref.shape[2])
        out_ref[n] = jnp.dot(mlp_ref[...], w_ref[:, cols], preferred_element_type=F32)


def mlp_out(place, mlp_hidden, w_out):
    rows, hidden = mlp_hidden.shape
    width = w_out.shape[1] // (2 * NZ)
    return call(
        mlp_out_kernel, [mlp_hidden, w_out], [((2 * NZ, rows, width), F32)], scalars=place,
        cost=4 * PER_US, name="mlp_out",
    )[0]


def mix_kernel(p0, p1, p2, p3, attn_ref):
    parts = (p0, p1, p2, p3)
    rows, width = attn_ref.shape
    for j in range(width // HD):
        cols = slice(j * HD, (j + 1) * HD)
        lses = [p[rows : rows + LSE_ROWS, cols].astype(F32) for p in parts]
        for i in range(rows // BLOCK):
            each = []
            for lse in lses:
                total = lse[4 * i : 4 * i + 1] + lse[4 * i + 1 : 4 * i + 2] + lse[4 * i + 2 : 4 * i + 3]
                each.append(total)
            top = functools.reduce(jnp.maximum, each)
            shares = [jnp.exp2(e - top) for e in each]
            scale = 1.0 / functools.reduce(jnp.add, shares)
            here = slice(i * BLOCK, (i + 1) * BLOCK)
            mixed = jnp.zeros((BLOCK, HD), F32)
            for share, p in zip(shares, parts):
                column = jnp.transpose(jnp.broadcast_to(share * scale, (BLOCK, BLOCK)))
                mixed = mixed + column * p[here, cols].astype(F32)
            attn_ref[here, cols] = mixed.astype(BF16)


def branch_kernel(place, *refs, chunks, mixing):
    refs = list(refs)
    if mixing:
        parts, (mlp_ref, w_ref, attn_ref), outs = refs[:SIDE], refs[SIDE : SIDE + 3], refs[SIDE + 3 :]
        mix_kernel(*parts, attn_ref)
    else:
        (attn_ref, mlp_ref, w_ref), outs = refs[:3], refs[3:]
    width = attn_ref.shape[1]
    for i, k in enumerate(chunks):
        for n, out_ref in ((NZ + k, outs[2 * i]), (k, outs[2 * i + 1])):
            cols = columns(place, n, width)
            acc = jnp.dot(attn_ref[...], w_ref[:, cols], preferred_element_type=F32) + mlp_ref[n]
            out_ref[...] = acc.astype(BF16)


def branch(place, inputs, mlp_branch, w_attn, chunks):
    _, rows, width = mlp_branch.shape
    mixing = len(inputs) == SIDE
    return call(
        functools.partial(branch_kernel, chunks=chunks, mixing=mixing),
        [*inputs, mlp_branch, w_attn], [((rows, width), BF16)] * (mixing + 2 * len(chunks)),
        scalars=place, name="branch",
    )


def chip_sum(send, keep):
    return keep.astype(F32) + other_core(send).astype(F32)


def finish_kernel(place, rows_ref, mine_ref, s1, s2, gate_ref, out_ref):
    count = place[2]
    for i in range(rows_ref.shape[0] // BLOCK):
        here = slice(i * BLOCK, (i + 1) * BLOCK)
        total = mine_ref[here, :] + s1[here, :].astype(F32) + s2[here, :].astype(F32)
        result = rows_ref[here, :].astype(F32) + gate_ref[...] * total
        out_ref[here, :] = jnp.where(i < count, result, 0.0).astype(BF16)


def finish(place, rows, mine, sums, gate):
    operands = [in_vmem(a) for a in (rows, mine, *sums, gate)]
    return pl.pallas_call(
        finish_kernel,
        in_specs=[spec(pltpu.SMEM)] + [spec(VMEM)] * len(operands),
        out_specs=spec(VMEM),
        out_shape=jax.ShapeDtypeStruct(rows.shape, BF16),
        compiler_params=pltpu.CompilerParams(vmem_limit_bytes=16 * 2**20),
        name="finish",
    )(place, *operands)


def partner(kind, at, core):
    if kind == "opposite":
        return (at + 2) % 4
    step = 1 if at % 2 == 0 else 3
    if (kind == "second") != (core == 1):
        step = 4 - step
    return (at + step) % 4


def along(axis, kind, a):
    pairs = []
    for y in range(4):
        for x in range(4):
            for h in range(8):
                core = h % 2
                if (axis == "a") == (core == 0):
                    to = partner(kind, y, core) * 4 + x
                else:
                    to = y * 4 + partner(kind, x, core)
                pairs.append(((y * 4 + x) * 8 + h, to * 8 + h))
    return lax.ppermute(a, ("patch", "head"), pairs)


def up_or_down(a, steps=(1, 3)):
    return lax.ppermute(
        a, "head", [(z * 2 + c, (z + steps[c]) % 4 * 2 + c) for z in range(4) for c in range(2)]
    )


def along_z(a, k):
    return lax.ppermute(a, "head", [(z * 2 + c, (z + k) % 4 * 2 + c) for z in range(4) for c in range(2)])


def other_core(a):
    return lax.ppermute(a, "head", [(i, i ^ 1) for i in range(8)])


def ring_near(axis, a):
    return [a, along(axis, "first", a), along(axis, "second", a)]


def ring_far(axis, buffers):
    return [*buffers, along(axis, "second", buffers[1])]


def body(
    hidden, key_cache, value_cache, block_order, refresh_counts, modulation,
    query_gain, key_gain, w_qkv, w_mlp, w_out_attn, w_out_mlp,
):
    count = refresh_counts[0]
    head = lax.axis_index("head")
    z, core = head // 2, head % 2
    place = jnp.stack([z, core, count]).astype(jnp.int32)
    ordered = jnp.concatenate([place, block_order[0, :RMAX]]).reshape(1, 3 + RMAX)
    width = hidden.shape[1]
    gate = lax.dynamic_slice(modulation, (2, head * width), (1, width))
    w_qkv = jnp.transpose(w_qkv, (1, 0, 2))

    rows, rest = pick(block_order, hidden, key_cache, value_cache)
    rest_first, rest_second = along("a", "first", rest), along("a", "second", rest)
    near, away = up_or_down(rows), up_or_down(rows, (3, 1))
    own = [rows, near, away, up_or_down(near)]
    pieces = own + [other_core(a) for a in own]
    pieces, rest_first, rest_second = lax.optimization_barrier((pieces, rest_first, rest_second))
    rest_opposite = along("a", "second", rest_first)

    query, fresh, modded = project(
        ordered, pieces, modulation, query_gain, key_gain, w_qkv, key_cache, value_cache
    )
    query, fresh, modded, rest_opposite = lax.optimization_barrier((query, fresh, modded, rest_opposite))
    rest = [rest, rest_first, rest_second, rest_opposite]
    queries, fresh = ring_near("b", query), ring_near("a", fresh)
    mlp_hidden = mlp_in(modded, w_mlp)
    queries, mlp_hidden = lax.optimization_barrier((queries, mlp_hidden))
    fresh = lax.optimization_barrier(fresh)
    queries, fresh = ring_far("b", queries), ring_far("a", fresh)
    state = attend(queries, rest)
    parts = attend(queries, fresh, state)
    kinds = ("first", "second", "opposite")
    back = [parts[0]] + [along("b", kind, parts[n + 1]) for n, kind in enumerate(kinds)]
    mlp_branch = mlp_out(place, mlp_hidden, w_out_mlp)
    attn, *pairs = branch(place, back, mlp_branch, w_out_attn, (0, 2))
    across, away = chip_sum(*pairs[:2]).astype(BF16), chip_sum(*pairs[2:]).astype(BF16)
    attn, across = lax.optimization_barrier((attn, across))
    across = up_or_down(across)
    near = chip_sum(*branch(place, [attn], mlp_branch, w_out_attn, (1,)))
    attn, across = lax.optimization_barrier((attn, across))
    near = up_or_down((near + across.astype(F32)).astype(BF16))
    mine = chip_sum(*branch(place, [attn], mlp_branch, w_out_attn, (3,)))
    return finish(place, rows, mine, [near, up_or_down(away, (3, 1))], gate)


def solution(mesh):
    in_specs = (
        P("patch", "head"), P("patch", "head"), P("patch", "head"), P("patch", None), P("patch"),
        P(), P(), P(),
        P(None, None, "head"), P(None, "head"), P("head", None), P("head", None),
    )
    return jax.shard_map(
        body, mesh=mesh, in_specs=in_specs, out_specs=P("patch", "head"), check_vma=False
    )
```

```python
import functools
import math

import jax
import jax.numpy as jnp
from jax import lax
from jax.experimental import pallas as pl
from jax.experimental.pallas import tpu as pltpu
from jax.sharding import PartitionSpec as P

HD = 128
BLOCK = 128
RMAX = 4
NZ = 4
SIDE = 4
LSE_ROWS = 16
NOTE_ROWS = 16
PER_US = 1_100_000_000
BF16 = jnp.bfloat16
F32 = jnp.float32
EXP2_SCALE = HD ** (-0.5) * math.log2(math.e)
VMEM = pltpu.VMEM


def spec(space):
    return pl.BlockSpec(memory_space=space)


def in_vmem(a):
    return pltpu.with_memory_space_constraint(a, VMEM)


def in_hbm(a):
    return pltpu.with_memory_space_constraint(a, pltpu.HBM)


def call(kernel, operands, outs, scalars=None, far=(), scratch=(), mib=16, cost=0, name=None):
    specs = [spec(VMEM)] * len(operands) + [spec(pltpu.HBM)] * len(far)
    operands = [in_vmem(a) for a in operands] + [in_hbm(a) for a in far]
    if scalars is not None:
        specs = [spec(pltpu.SMEM)] + specs
        operands = [scalars] + operands
    return pl.pallas_call(
        kernel,
        in_specs=specs,
        out_specs=[spec(VMEM)] * len(outs),
        out_shape=[VMEM(shape, dtype) for shape, dtype in outs],
        scratch_shapes=list(scratch),
        compiler_params=pltpu.CompilerParams(vmem_limit_bytes=mib * 2**20),
        cost_estimate=pl.CostEstimate(flops=cost, bytes_accessed=1000, transcendentals=0),
        name=name,
    )(*operands)


def copies_of(pairs, sems):
    copies = [pltpu.make_async_copy(src, dst, sems.at[n]) for n, (src, dst) in enumerate(pairs)]
    for copy in copies:
        copy.start()
    return copies


def block_at(order, place):
    return pl.ds(pl.multiple_of(order[0, place] * BLOCK, BLOCK), BLOCK)


def pick_kernel(order, hidden, keys, values, rows_ref, rest_ref, sems):
    pairs = []
    width = keys.shape[1]
    for i in range(RMAX):
        pairs.append((hidden.at[block_at(order, i), :], rows_ref.at[pl.ds(i * BLOCK, BLOCK), :]))
    for i in range(RMAX):
        here, to = block_at(order, RMAX + i), pl.ds(i * BLOCK, BLOCK)
        for n, ref in enumerate((keys, values)):
            pairs.append((ref.at[here, :], rest_ref.at[to, pl.ds(n * width, width)]))
    for copy in copies_of(pairs, sems):
        copy.wait()


def pick(order, hidden, keys, values):
    tall, width = RMAX * BLOCK, hidden.shape[1]
    return call(
        pick_kernel, [], [((tall, width), BF16), ((tall, 2 * width), BF16)], scalars=in_hbm(order),
        far=[hidden, keys, values], scratch=[pltpu.SemaphoreType.DMA((3 * RMAX,))], name="pick",
    )


def project_kernel(
    place, p0, p1, p2, p3, p4, p5, p6, p7, mod_far, qg_far, kg_far, w_ref, keys, values,
    q_ref, kv_ref, modded_ref, pieces_ref, old_ref, mod_ref, qg_ref, kg_ref, w_vmem, sems,
):
    z, core, count = place[0, 0], place[0, 1], place[0, 2]
    rows, width = p0.shape
    far_pieces = (p1, p2, p3, p4, p5, p6, p7)
    pieces = [p0] + [pieces_ref.at[n] for n in range(len(far_pieces))]
    features = width * len(pieces)
    copies = copies_of(
        [(ref, pieces_ref.at[n]) for n, ref in enumerate(far_pieces)]
        + [(mod_far, mod_ref), (qg_far, qg_ref), (kg_far, kg_ref)]
        + [(w_ref.at[n], w_vmem.at[n]) for n in range(3)]
        + [
            (ref.at[block_at(place, 3 + i), :], old_ref.at[pl.ds(i * BLOCK, BLOCK), pl.ds(n * width, width)])
            for i in range(RMAX)
            for n, ref in enumerate((keys, values))
        ],
        sems,
    )
    piece_copies, (mod_copy, qg_copy, kg_copy), weight_copies, old_copies = (
        copies[:7], copies[7:10], copies[10:13], copies[13:],
    )
    near = lax.rem(z + NZ - 1 + 2 * core, NZ)
    away = lax.rem(z + NZ + 1 - 2 * core, NZ)
    across = lax.rem(z + 2, NZ)
    homes = [zone * 2 + core for zone in (z, near, away, across)]
    homes += [zone * 2 + 1 - core for zone in (z, away, near, across)]
    for copy in (*piece_copies, mod_copy):
        copy.wait()
    tall = 32

    def norm(i, carry):
        here = pl.ds(pl.multiple_of(i * tall, tall), tall)
        total = jnp.zeros((tall, width), F32)
        for n in range(8):
            total = total + pieces[n][here, :].astype(F32)
        mean = jnp.sum(total, axis=-1, keepdims=True) * (1.0 / features)
        square = jnp.zeros((tall, width), F32)
        for n in range(8):
            center = pieces[n][here, :].astype(F32) - mean
            square = square + center * center
        spread = jnp.sum(square, axis=-1, keepdims=True) * (1.0 / features)
        inv = lax.rsqrt(spread + 1e-06)
        for n, h in enumerate(homes):
            cols = pl.ds(pl.multiple_of(h * width, 128), width)
            normed = (pieces[n][here, :].astype(F32) - mean) * inv
            out = normed * (1.0 + mod_ref[1:2, cols]) + mod_ref[0:1, cols]
            modded_ref[here, cols] = out.astype(BF16)
        return carry

    lax.fori_loop(0, rows // tall, norm, 0, unroll=2)

    def rms(v, gain):
        scale = lax.rsqrt(jnp.mean(v * v, axis=-1, keepdims=True) + 1e-06)
        return v * scale * gain

    heads = width // HD
    waits = {0: [weight_copies[0], qg_copy, kg_copy], 2: [weight_copies[1], *old_copies], 6: [weight_copies[2]]}
    for first in range(0, 3 * heads, 2):
        pair = range(first, min(first + 2, 3 * heads))
        for copy in waits.get(first, ()):
            copy.wait()
        for i in range(rows // 256):
            here = slice(i * 256, (i + 1) * 256)
            weights = [w_vmem[h // heads][:, h % heads * HD : (h % heads + 1) * HD] for h in pair]
            acc = jnp.dot(
                modded_ref[here, :], jnp.concatenate(weights, axis=1), preferred_element_type=F32
            )
            live = i * 256 + lax.broadcasted_iota(jnp.int32, (256, HD), 0) < count * BLOCK
            for n, h in enumerate(pair):
                v = acc[:, n * HD : (n + 1) * HD]
                if h < heads:
                    q_ref[here, h * HD : (h + 1) * HD] = rms(v, qg_ref[...]).astype(BF16)
                else:
                    cols = slice((h - heads) * HD, (h - heads + 1) * HD)
                    v = rms(v, kg_ref[...]) if h < 2 * heads else v
                    kv_ref[here, cols] = jnp.where(live, v, old_ref[here, cols].astype(F32)).astype(BF16)
    q_ref[rows : rows + NOTE_ROWS, :] = (
        jnp.full((NOTE_ROWS, width), count, jnp.int32).astype(F32).astype(BF16)
    )


def project(place, pieces, modulation, query_gain, key_gain, w_qkv, keys, values):
    rows, width = pieces[0].shape
    features = w_qkv.shape[1]
    return call(
        project_kernel,
        pieces[:1],
        [((rows + NOTE_ROWS, width), BF16), ((rows, 2 * width), BF16), ((rows, features), BF16)],
        scalars=place, far=[
            *pieces[1:], modulation, query_gain.reshape(1, HD), key_gain.reshape(1, HD), w_qkv, keys, values,
        ],
        scratch=[
            VMEM((7, rows, width), BF16), VMEM((rows, 2 * width), BF16),
            VMEM(modulation.shape, F32), VMEM((1, HD), F32), VMEM((1, HD), F32), VMEM(w_qkv.shape, BF16),
            pltpu.SemaphoreType.DMA((13 + 2 * RMAX,)),
        ],
        cost=10 * PER_US, mib=24, name="project",
    )


def mlp_kernel(modded_ref, w_ref, out_ref, w_vmem, sems):
    width = w_ref.shape[1] // 3
    tiles = [slice(j * width, (j + 1) * width) for j in range(3)]
    copies = copies_of(
        [(w_ref.at[:, pl.ds(j * width, width)], w_vmem.at[j]) for j in range(3)], sems
    )
    for j in range(3):
        copies[j].wait()
        for i in range(modded_ref.shape[0] // 256):
            here = slice(i * 256, (i + 1) * 256)
            acc = jnp.dot(modded_ref[here, :], w_vmem[j], preferred_element_type=F32)
            out_ref[here, tiles[j]] = jax.nn.gelu(acc, approximate=True).astype(BF16)


def mlp_in(modded, w_mlp):
    rows, features = modded.shape
    hidden = w_mlp.shape[1]
    return call(
        mlp_kernel, [modded], [((rows, hidden), BF16)], far=[w_mlp],
        scratch=[VMEM((3, features, hidden // 3), BF16), pltpu.SemaphoreType.DMA((3,))],
        cost=8 * PER_US, name="mlp_in",
    )[0]


def attend_kernel(*refs, n_keys, chained):
    refs = list(refs)

    def take(n):
        out = refs[:n]
        del refs[:n]
        return out

    q_refs, kv_refs = take(SIDE), take(n_keys)
    o_in, lse_in = take(2) if chained else (None, None)
    out_refs = take(SIDE) if chained else None
    o_out, lse_out, qs = take(3)
    rows, width = q_refs[0].shape[0] - NOTE_ROWS, q_refs[0].shape[1]
    slots, heads = rows // BLOCK, width // HD

    starts, live, total = [], [], 0
    for s in range(SIDE):
        count = jnp.max(q_refs[s][rows : rows + NOTE_ROWS, :HD].astype(F32)).astype(jnp.int32)
        starts.append(total)
        live.append(count)
        total = total + count

    for s in range(SIDE):
        for i in range(slots):
            @pl.when(i < live[s])
            def _(s=s, i=i):
                to = pl.ds(pl.multiple_of((starts[s] + i) * BLOCK, BLOCK), BLOCK)
                qs[to, :] = q_refs[s][i * BLOCK : (i + 1) * BLOCK, :]

    def lanes(j):
        return slice(j * HD, (j + 1) * HD)

    def tile(at, tall):
        here = pl.ds(pl.multiple_of(at * BLOCK, BLOCK), tall)

        def score(j):
            q = qs[here, lanes(j)]
            return [
                lax.dot_general(q, kv[:, lanes(j)], (((1,), (1,)), ((), ())), preferred_element_type=F32)
                for kv in kv_refs
            ]

        ahead = score(0)
        for j in range(heads):
            scores = ahead
            if j + 1 < heads:
                ahead = score(j + 1)
            top = functools.reduce(jnp.maximum, [jnp.max(s, axis=-1, keepdims=True) for s in scores])
            top = top * EXP2_SCALE
            if chained:
                lse = lse_in[here, lanes(j)]
                top = jnp.maximum(top, lse[:, :1])
                share = jnp.exp2(lse - top)
                acc = jnp.concatenate([o_in[here, lanes(j)] * share, share], axis=1)
            else:
                acc = jnp.zeros((tall, 2 * HD), F32)
            for s, kv in zip(scores, kv_refs):
                weights = jnp.exp2(s * EXP2_SCALE - top).astype(BF16)
                value = kv[:, width + j * HD : width + (j + 1) * HD]
                value = jnp.concatenate([value, jnp.ones(value.shape, BF16)], axis=1)
                acc = acc + jnp.dot(weights, value, preferred_element_type=F32)
            o_out[here, lanes(j)] = acc[:, :HD] / acc[:, HD:]
            lse_out[here, lanes(j)] = top + jnp.log2(acc[:, HD:])

    big = lax.div(total, 4)
    done = 4 * big

    def tall_tile(t, carry):
        tile(4 * t, 4 * BLOCK)
        return carry

    def short_tile(t, carry):
        tile(done + 2 * t, 2 * BLOCK)
        return carry

    lax.fori_loop(0, big, tall_tile, 0)
    lax.fori_loop(0, lax.div(total - done + 1, 2), short_tile, 0)
    if not chained:
        return

    line = lax.broadcasted_iota(jnp.int32, (LSE_ROWS, BLOCK), 0)
    for s in range(SIDE):
        out_refs[s][rows : rows + LSE_ROWS, :] = jnp.zeros((LSE_ROWS, width), BF16)
        for i in range(slots):
            @pl.when(i < live[s])
            def _(s=s, i=i):
                here = pl.ds(pl.multiple_of((starts[s] + i) * BLOCK, BLOCK), BLOCK)
                out_refs[s][i * BLOCK : (i + 1) * BLOCK, :] = o_out[here, :].astype(BF16)
                for j in range(heads):
                    lse = jnp.transpose(lse_out[here, lanes(j)])[:LSE_ROWS, :]
                    high = lse.astype(BF16).astype(F32)
                    mid = (lse - high).astype(BF16).astype(F32)
                    low = lse - high - mid
                    packed = out_refs[s][rows : rows + LSE_ROWS, lanes(j)].astype(F32)
                    part = line - 4 * i
                    packed = jnp.where(part == 0, high, packed)
                    packed = jnp.where(part == 1, mid, packed)
                    packed = jnp.where(part == 2, low, packed)
                    out_refs[s][rows : rows + LSE_ROWS, lanes(j)] = packed.astype(BF16)


def attend(queries, caches, state=()):
    tall, width = queries[0].shape
    rows = tall - NOTE_ROWS
    most = SIDE * rows + BLOCK
    states = [((most, width), F32)] * 2
    scratch = [VMEM((most, width), BF16)]
    if state:
        outs = [((rows + LSE_ROWS, width), BF16)] * SIDE
        scratch = [VMEM(shape, dtype) for shape, dtype in states] + scratch
    else:
        outs = states
    return call(
        functools.partial(attend_kernel, n_keys=len(caches), chained=bool(state)),
        [*queries, *caches, *state], outs, scratch=scratch, mib=24, cost=9 * PER_US if state else 5 * PER_US,
        name="attend_last" if state else "attend_first",
    )


CHUNKS = ("across", "near", "away", "own")


def columns(place, n, width):
    z, core = place[0], place[1]
    step = lax.rem(1 + 2 * core, NZ)
    if n >= NZ:
        step = NZ - step
    zone = lax.rem(z + (2, step, NZ - step, 0)[n % NZ], NZ)
    side = core if n < NZ else 1 - core
    return pl.ds(pl.multiple_of((zone * 2 + side) * width, 128), width)


def mlp_out_kernel(place, mlp_ref, w_ref, out_ref):
    for n in range(2 * NZ):
        cols = columns(place, n, out_ref.shape[2])
        out_ref[n] = jnp.dot(mlp_ref[...], w_ref[:, cols], preferred_element_type=F32)


def mlp_out(place, mlp_hidden, w_out):
    rows, hidden = mlp_hidden.shape
    width = w_out.shape[1] // (2 * NZ)
    return call(
        mlp_out_kernel, [mlp_hidden, w_out], [((2 * NZ, rows, width), F32)], scalars=place,
        cost=4 * PER_US, name="mlp_out",
    )[0]


def mix_kernel(p0, p1, p2, p3, attn_ref):
    parts = (p0, p1, p2, p3)
    rows, width = attn_ref.shape
    for j in range(width // HD):
        cols = slice(j * HD, (j + 1) * HD)
        lses = [p[rows : rows + LSE_ROWS, cols].astype(F32) for p in parts]
        for i in range(rows // BLOCK):
            each = []
            for lse in lses:
                total = lse[4 * i : 4 * i + 1] + lse[4 * i + 1 : 4 * i + 2] + lse[4 * i + 2 : 4 * i + 3]
                each.append(total)
            top = functools.reduce(jnp.maximum, each)
            shares = [jnp.exp2(e - top) for e in each]
            scale = 1.0 / functools.reduce(jnp.add, shares)
            here = slice(i * BLOCK, (i + 1) * BLOCK)
            mixed = jnp.zeros((BLOCK, HD), F32)
            for share, p in zip(shares, parts):
                column = jnp.transpose(jnp.broadcast_to(share * scale, (BLOCK, BLOCK)))
                mixed = mixed + column * p[here, cols].astype(F32)
            attn_ref[here, cols] = mixed.astype(BF16)


def branch_kernel(place, *refs, chunks, mixing):
    refs = list(refs)
    if mixing:
        parts, (mlp_ref, w_ref, attn_ref), outs = refs[:SIDE], refs[SIDE : SIDE + 3], refs[SIDE + 3 :]
        mix_kernel(*parts, attn_ref)
    else:
        (attn_ref, mlp_ref, w_ref), outs = refs[:3], refs[3:]
    width = attn_ref.shape[1]
    for i, k in enumerate(chunks):
        for n, out_ref in ((NZ + k, outs[2 * i]), (k, outs[2 * i + 1])):
            cols = columns(place, n, width)
            acc = jnp.dot(attn_ref[...], w_ref[:, cols], preferred_element_type=F32) + mlp_ref[n]
            out_ref[...] = acc.astype(BF16)


def branch(place, inputs, mlp_branch, w_attn, chunks):
    _, rows, width = mlp_branch.shape
    mixing = len(inputs) == SIDE
    return call(
        functools.partial(branch_kernel, chunks=chunks, mixing=mixing),
        [*inputs, mlp_branch, w_attn], [((rows, width), BF16)] * (mixing + 2 * len(chunks)),
        scalars=place, name="branch",
    )


def chip_sum(send, keep):
    return keep.astype(F32) + other_core(send).astype(F32)


def finish_kernel(place, rows_ref, mine_ref, s1, s2, gate_ref, out_ref):
    count = place[2]
    for i in range(rows_ref.shape[0] // BLOCK):
        here = slice(i * BLOCK, (i + 1) * BLOCK)
        total = mine_ref[here, :] + s1[here, :].astype(F32) + s2[here, :].astype(F32)
        result = rows_ref[here, :].astype(F32) + gate_ref[...] * total
        out_ref[here, :] = jnp.where(i < count, result, 0.0).astype(BF16)


def finish(place, rows, mine, sums, gate):
    operands = [in_vmem(a) for a in (rows, mine, *sums, gate)]
    return pl.pallas_call(
        finish_kernel,
        in_specs=[spec(pltpu.SMEM)] + [spec(VMEM)] * len(operands),
        out_specs=spec(VMEM),
        out_shape=jax.ShapeDtypeStruct(rows.shape, BF16),
        compiler_params=pltpu.CompilerParams(vmem_limit_bytes=16 * 2**20),
        name="finish",
    )(place, *operands)


def partner(kind, at, core):
    if kind == "opposite":
        return (at + 2) % 4
    step = 1 if at % 2 == 0 else 3
    if (kind == "second") != (core == 1):
        step = 4 - step
    return (at + step) % 4


def along(axis, kind, a):
    pairs = []
    for y in range(4):
        for x in range(4):
            for h in range(8):
                core = h % 2
                if (axis == "a") == (core == 0):
                    to = partner(kind, y, core) * 4 + x
                else:
                    to = y * 4 + partner(kind, x, core)
                pairs.append(((y * 4 + x) * 8 + h, to * 8 + h))
    return lax.ppermute(a, ("patch", "head"), pairs)


def up_or_down(a, steps=(1, 3)):
    return lax.ppermute(
        a, "head", [(z * 2 + c, (z + steps[c]) % 4 * 2 + c) for z in range(4) for c in range(2)]
    )


def along_z(a, k):
    return lax.ppermute(a, "head", [(z * 2 + c, (z + k) % 4 * 2 + c) for z in range(4) for c in range(2)])


def other_core(a):
    return lax.ppermute(a, "head", [(i, i ^ 1) for i in range(8)])


def ring_near(axis, a):
    return [a, along(axis, "first", a), along(axis, "second", a)]


def ring_far(axis, buffers):
    return [*buffers, along(axis, "second", buffers[1])]


def body(
    hidden, key_cache, value_cache, block_order, refresh_counts, modulation,
    query_gain, key_gain, w_qkv, w_mlp, w_out_attn, w_out_mlp,
):
    count = refresh_counts[0]
    head = lax.axis_index("head")
    z, core = head // 2, head % 2
    place = jnp.stack([z, core, count]).astype(jnp.int32)
    ordered = jnp.concatenate([place, block_order[0, :RMAX]]).reshape(1, 3 + RMAX)
    width = hidden.shape[1]
    gate = lax.dynamic_slice(modulation, (2, head * width), (1, width))
    w_qkv = jnp.transpose(w_qkv, (1, 0, 2))

    rows, rest = pick(block_order, hidden, key_cache, value_cache)
    rest_first, rest_second = along("a", "first", rest), along("a", "second", rest)
    near, away = up_or_down(rows), up_or_down(rows, (3, 1))
    own = [rows, near, away, up_or_down(near)]
    pieces = own + [other_core(a) for a in own]
    pieces, rest_first, rest_second = lax.optimization_barrier((pieces, rest_first, rest_second))
    rest_opposite = along("a", "second", rest_first)

    query, fresh, modded = project(
        ordered, pieces, modulation, query_gain, key_gain, w_qkv, key_cache, value_cache
    )
    query, fresh, modded, rest_opposite = lax.optimization_barrier((query, fresh, modded, rest_opposite))
    rest = [rest, rest_first, rest_second, rest_opposite]
    queries, fresh = ring_near("b", query), ring_near("a", fresh)
    mlp_hidden = mlp_in(modded, w_mlp)
    queries, mlp_hidden = lax.optimization_barrier((queries, mlp_hidden))
    fresh = lax.optimization_barrier(fresh)
    queries, fresh = ring_far("b", queries), ring_far("a", fresh)
    state = attend(queries, rest)
    parts = attend(queries, fresh, state)
    kinds = ("first", "second", "opposite")
    back = [parts[0]] + [along("b", kind, parts[n + 1]) for n, kind in enumerate(kinds)]
    mlp_branch = mlp_out(place, mlp_hidden, w_out_mlp)
    attn, *pairs = branch(place, back, mlp_branch, w_out_attn, (0, 2))
    across, away = chip_sum(*pairs[:2]).astype(BF16), chip_sum(*pairs[2:]).astype(BF16)
    attn, across = lax.optimization_barrier((attn, across))
    across = up_or_down(across)
    near = chip_sum(*branch(place, [attn], mlp_branch, w_out_attn, (1,)))
    attn, across = lax.optimization_barrier((attn, across))
    near = up_or_down((near + across.astype(F32)).astype(BF16))
    mine = chip_sum(*branch(place, [attn], mlp_branch, w_out_attn, (3,)))
    return finish(place, rows, mine, [near, up_or_down(away, (3, 1))], gate)


def solution(mesh):
    in_specs = (
        P("patch", "head"), P("patch", "head"), P("patch", "head"), P("patch", None), P("patch"),
        P(), P(), P(),
        P(None, None, "head"), P(None, "head"), P("head", None), P("head", None),
    )
    return jax.shard_map(
        body, mesh=mesh, in_specs=in_specs, out_specs=P("patch", "head"), check_vma=False
    )
```
